32 devices in a mesh: band: 8 (over y, x, core), head: 4 (over z).
Axes of the slice: x: 2, y: 2, z: 4, core: 2. Of those that a mesh axis runs over, the one named last changes fastest.
Arguments:
- queries: bfloat16 [256, 8192], P('head', 'band'), may hold values from -76 to 76
- keys: bfloat16 [256, 8192], P('head', 'band'), may hold values from -6 to 6
- values: bfloat16 [256, 8192], P('head', 'band'), may hold values from -6 to 6
- grad_out: bfloat16 [256, 8192], P('head', 'band'), may hold values from -6 to 6
- w_out: bfloat16 [256, 256], P('head'), may hold values from -0.375 to 0.375
- key_lists: int32 [64, 8], P('band'), may hold values from 0 to 63, as said below
- key_counts: int32 [64], P('band'), may hold values from 2 to 8, as said below
Outputs:
- grad_queries: bfloat16 [256, 8192], P('head', 'band')
- grad_keys: bfloat16 [256, 8192], P('head', 'band')
- grad_values: bfloat16 [256, 8192], P('head', 'band')
- grad_w_out: float32 [256, 256], P('head')
The draws below stay inside these ranges and needn't reach their ends.
Inputs may be any that keep to these rules, and one draw needn't show every extreme that they name: `key_lists`: row b holds 8 different blocks; the first is b itself and every entry lies within 8 blocks of b. `key_counts`: the number of leading entries of the row of key_lists that are used.
All inputs are finite; a program needn't handle non-finite values.
Results may differ from the reference program's by a relative error of at most 0.0058.
Values may be sent and summed in bfloat16 or wider, within the bound.
No kernel may reach another device: no remote copies, remote signals or barrier semaphores. Data moves between devices by JAX's collectives and lax.ppermute only.
A program may use at most 64 MiB of HBM per device.

```python
import jax
import jax.numpy as jnp
from jax import lax

D = 256
HEADS = 8
HEAD_DIM = 32
BLOCK = 128
REACH = 4
MAX_KEYS = 8
MIN_KEYS = 2
TOKENS = 8192
KEY_BLOCKS = 64


def shared_fields(key):
    key_seed = jax.random.fold_in(key, 101)
    query_seed = jax.random.fold_in(key, 102)
    key_field = jnp.clip(jax.random.normal(key_seed, (TOKENS, D), jnp.float32), -6.0, 6.0)
    query_field = jnp.clip(jax.random.normal(query_seed, (TOKENS, D), jnp.float32), -6.0, 6.0)
    return (query_field, key_field)


def draw_queries(key, part):
    query_field, key_field = shared_fields(key)
    return query_field.T.astype(jnp.bfloat16)


def draw_keys(key, part):
    query_field, key_field = shared_fields(key)
    return key_field.T.astype(jnp.bfloat16)


def draw_key_lists(key, part):
    block_index = jnp.arange(KEY_BLOCKS, dtype=jnp.int32)
    window_low = jnp.clip(block_index - REACH, 0, KEY_BLOCKS - 1 - 2 * REACH)
    rank_seed = jax.random.fold_in(key, 201)
    scores = jax.random.randint(rank_seed, (KEY_BLOCKS, 2 * REACH), 0, 2 ** 20) * (2 * REACH) + jnp.arange(2 * REACH, dtype=jnp.int32)
    ranking = jnp.argsort(scores, axis=1).astype(jnp.int32)
    chosen = ranking[:, :MAX_KEYS - 1]
    offset = block_index - window_low
    others = window_low[:, None] + chosen + (chosen >= offset[:, None]).astype(jnp.int32)
    return jnp.concatenate([block_index[:, None], others], axis=1).astype(jnp.int32)


def draw_key_counts(key, part):
    block_index = jnp.arange(KEY_BLOCKS, dtype=jnp.int32)
    distance = jnp.minimum(block_index, KEY_BLOCKS - 1 - block_index)
    baseline = MAX_KEYS - (MAX_KEYS - MIN_KEYS) * 2 * distance // KEY_BLOCKS
    jitter = jax.random.randint(jax.random.fold_in(key, 301), (KEY_BLOCKS,), 0, 2) * (distance > 0).astype(jnp.int32)
    return jnp.clip(baseline - jitter, MIN_KEYS, MAX_KEYS).astype(jnp.int32)


def levels(rng, shape, split, smallest, largest):
    def one(axis_at, blocks):
        draws = jax.random.uniform(jax.random.fold_in(jax.random.fold_in(rng, 6), axis_at), (blocks,), jnp.float32, smallest / len(split), largest / len(split))
        return jnp.repeat(jnp.exp(draws), shape[axis_at] // blocks).reshape((-1,) + (1,) * (len(shape) - axis_at - 1))

    factor_of = one(*split[0])
    for cut in split[1:]:
        factor_of = factor_of * one(*cut)
    return factor_of


def centred(own_key, dims, scale, reach, shards=(), held_as=jnp.bfloat16):
    level = levels(own_key, dims, shards, -0.22, 0.18) if shards else 1.0
    values = jax.random.normal(own_key, dims, jnp.float32) * scale * level
    return jnp.minimum(jnp.maximum(values, -reach), reach).astype(held_as)


def setup_inputs(seed: int = 0) -> dict:
    streams_of = jax.random.split(jax.random.key(seed), 8)
    return {
        "queries": draw_queries(jax.random.fold_in(streams_of[7], 71), 0),
        "keys": draw_keys(jax.random.fold_in(streams_of[7], 71), 0),
        "values": centred(streams_of[2], (D, TOKENS), 1.0, 6.0, ((0, 4), (1, 8))),
        "grad_out": centred(streams_of[3], (D, TOKENS), 1.0, 6.0, ((0, 4), (1, 8))),
        "w_out": centred(streams_of[4], (D, D), D ** -0.5, 0.375, ((0, 4),)),
        "key_lists": draw_key_lists(jax.random.fold_in(streams_of[7], 71), 0),
        "key_counts": draw_key_counts(jax.random.fold_in(streams_of[7], 71), 0),
    }


def block_terms(query, grad, picked_k, picked_v, bias, live):
    scale = HEAD_DIM ** -0.5
    scores = jnp.einsum("qhd,khd->hqk", query, picked_k) * scale + bias
    scores = jnp.where(live, scores, -jnp.inf)
    peak = jnp.max(scores, axis=-1)
    log_total = peak + jnp.log(jnp.sum(jnp.exp(scores - peak[..., None]), axis=-1))
    probs = jnp.exp(scores - log_total[..., None])
    probs_low = lax.optimization_barrier(probs.astype(jnp.bfloat16)).astype(jnp.float32)
    dprobs = jnp.einsum("qhd,khd->hqk", grad, picked_v)
    spread = jnp.sum(probs * dprobs, axis=-1)
    dscores = (probs * (dprobs - spread[..., None]) * scale).astype(jnp.bfloat16)
    dscores = lax.optimization_barrier(dscores).astype(jnp.float32)
    dquery = jnp.einsum("hqk,khd->qhd", dscores, picked_k)
    dkey = jnp.einsum("hqk,qhd->khd", dscores, query)
    dvalue = jnp.einsum("hqk,qhd->khd", probs_low, grad)
    attended = jnp.einsum("hqk,khd->qhd", probs_low, picked_v)
    return dquery, dkey, dvalue, attended


def reference(queries, keys, values, grad_out, w_out, key_lists, key_counts):
    tokens = queries.shape[1]
    blocks = tokens // BLOCK
    grad_att = jnp.dot(w_out, grad_out, preferred_element_type=jnp.float32).astype(jnp.bfloat16).T
    positions = jnp.arange(tokens, dtype=jnp.int32).astype(jnp.float32)
    logw = jnp.log(jnp.sin(jnp.pi * (positions + 0.5) / tokens)).reshape(blocks, BLOCK)
    shape4 = (blocks, BLOCK, HEADS, HEAD_DIM)
    query_all = queries.T.reshape(shape4)
    key_all = keys.T.reshape(shape4)
    value_all = values.T.reshape(shape4)
    grad_all = grad_att.reshape(shape4)
    slot_ids = jnp.arange(MAX_KEYS, dtype=jnp.int32)
    span = MAX_KEYS * BLOCK

    def step(carry, block_id):
        acc_k, acc_v = carry
        slots = key_lists[block_id].astype(jnp.int32)
        live = jnp.repeat(slot_ids < key_counts[block_id], BLOCK)
        picked_k = key_all[slots].astype(jnp.float32).reshape(span, HEADS, HEAD_DIM)
        picked_v = value_all[slots].astype(jnp.float32).reshape(span, HEADS, HEAD_DIM)
        bias = logw[slots].reshape(span)
        query = query_all[block_id].astype(jnp.float32)
        grad = grad_all[block_id].astype(jnp.float32)
        dquery, dkey, dvalue, attended = block_terms(query, grad, picked_k, picked_v, bias, live)
        acc_k = acc_k.at[slots].add(dkey.reshape(MAX_KEYS, BLOCK, D))
        acc_v = acc_v.at[slots].add(dvalue.reshape(MAX_KEYS, BLOCK, D))
        return (acc_k, acc_v), (dquery.reshape(BLOCK, D).astype(jnp.bfloat16), attended.reshape(BLOCK, D).astype(jnp.bfloat16))

    zeros = jnp.zeros((blocks, BLOCK, D), jnp.float32)
    (acc_k, acc_v), (dq_blocks, att_blocks) = lax.scan(step, (zeros, zeros), jnp.arange(blocks, dtype=jnp.int32))
    grad_queries = dq_blocks.reshape(tokens, D).T
    grad_keys = acc_k.reshape(tokens, D).astype(jnp.bfloat16).T
    grad_values = acc_v.reshape(tokens, D).astype(jnp.bfloat16).T
    attended = att_blocks.reshape(tokens, D)
    grad_w_out = jnp.dot(attended.T, grad_out.T, preferred_element_type=jnp.float32)
    return (grad_queries, grad_keys, grad_values, grad_w_out)
```

```python
import functools

import jax
import jax.numpy as jnp
from jax import lax
from jax.experimental import pallas as pl
from jax.experimental.pallas import tpu as pltpu
from jax.sharding import PartitionSpec as P

HEAD_DIM = 32
BLOCK = 128
REACH = 4
MAX_KEYS = 8
RIM = 2 * REACH
SCALE = HEAD_DIM ** (-0.5)
LOG2E = 1.4426950408889634
RAW = SCALE * LOG2E
MASKED = -1e30
AUG = 16
F32 = jnp.float32
BF16 = jnp.bfloat16
VMEM_LIMIT = 48 * 1024 * 1024


def dot(a, b):
    return lax.dot_general(a, b, (((1,), (0,)), ((), ())), preferred_element_type=F32)


def dot_nt(a, b):
    return lax.dot_general(a, b, (((1,), (1,)), ((), ())), preferred_element_type=F32)


def split3(x):
    hi = x.astype(BF16).astype(F32)
    rest = x - hi
    mid = rest.astype(BF16).astype(F32)
    return hi, mid, (rest - mid).astype(BF16).astype(F32)


def aug_rows(rows, width):
    at = lax.broadcasted_iota(jnp.int32, (AUG, width), 0)
    out = jnp.zeros((AUG, width), F32)
    for i, row in enumerate(rows):
        out = jnp.where(at == i, row, out)
    return out.astype(BF16)


def spread_heads(x, heads):
    zero = jnp.zeros((HEAD_DIM, BLOCK), x.dtype)
    rows = []
    for h in range(heads):
        part = x[h * HEAD_DIM : (h + 1) * HEAD_DIM]
        rows.append(jnp.concatenate([part if g == h else zero for g in range(heads)], axis=1))
    return jnp.concatenate(rows, axis=0)


def pick_heads(x, heads):
    return jnp.concatenate(
        [
            x[h * HEAD_DIM : (h + 1) * HEAD_DIM, h * BLOCK : (h + 1) * BLOCK]
            for h in range(heads)
        ],
        axis=0,
    )


def slot_of(lists_ref, counts_ref, row, j, first_block, ext):
    return jnp.where(j < counts_ref[row], lists_ref[row, j] - first_block, ext)


def lane_block(i):
    return pl.ds(pl.multiple_of(i * BLOCK, BLOCK), BLOCK)


def attend_kernel(
    total, lists_ref, counts_ref, q_ref, k_ref, v_ref, lo_ref, hi_ref,
    ka_ref, va_ref, kn_ref, att_ref, t_ref, vn_ref, s_ref,
):
    chans = q_ref.shape[0]
    heads = chans // HEAD_DIM
    blocks = q_ref.shape[1] // BLOCK
    ext = blocks + 2 * RIM
    width = heads * BLOCK
    first_block = lax.axis_index("band") * blocks - RIM

    at = lax.broadcasted_iota(jnp.int32, (ext, BLOCK), 0) * BLOCK
    at = at + lax.broadcasted_iota(jnp.int32, (ext, BLOCK), 1) + first_block * BLOCK
    at = jnp.clip(at, 0, total - 1).astype(F32)
    logw = jnp.log(jnp.sin(jnp.pi * (at + 0.5) / total))
    hi, mid, low = split3(logw * (1.0 / SCALE))
    pad = jnp.zeros((BLOCK - chans - AUG, BLOCK), BF16)
    v_aug = aug_rows([1.0, 1.0, 1.0], BLOCK)
    for b in range(ext + 1):
        if b == ext:
            k_blk = jnp.zeros((chans, BLOCK), BF16)
            v_blk = k_blk
            k_aug = aug_rows([MASKED, 0.0, 0.0, 1.0, 1.0, 1.0], BLOCK)
        else:
            if b < RIM:
                at_lanes = slice(b * BLOCK, (b + 1) * BLOCK)
                k_blk, v_blk = lo_ref[0, :, at_lanes], lo_ref[1, :, at_lanes]
            elif b < RIM + blocks:
                at_lanes = slice((b - RIM) * BLOCK, (b - RIM + 1) * BLOCK)
                k_blk, v_blk = k_ref[:, at_lanes], v_ref[:, at_lanes]
            else:
                at_lanes = slice((b - RIM - blocks) * BLOCK, (b - RIM - blocks + 1) * BLOCK)
                k_blk, v_blk = hi_ref[0, :, at_lanes], hi_ref[1, :, at_lanes]
            k_aug = aug_rows(
                [hi[b : b + 1], mid[b : b + 1], low[b : b + 1], 1.0, 1.0, 1.0], BLOCK
            )
        kn_ref[b] = k_blk
        v_with = jnp.concatenate([v_blk, v_aug], axis=0)
        vn_ref[b] = v_with
        ka_ref[b] = jnp.concatenate([k_blk, k_aug, pad], axis=0).T
        va_ref[b] = jnp.concatenate([v_with, pad], axis=0).T

    ones = aug_rows([1.0, 1.0, 1.0], width)
    pad_w = jnp.zeros((BLOCK - chans - AUG, width), BF16)

    def body(i, carry):
        q_aug = jnp.concatenate([spread_heads(q_ref[:, lane_block(i)], heads), ones, pad_w], axis=0)
        slots = [slot_of(lists_ref, counts_ref, i, j, first_block, ext) for j in range(MAX_KEYS)]
        peak = None
        for j in range(MAX_KEYS):
            s = dot(ka_ref[slots[j]], q_aug)
            s_ref[j * BLOCK : (j + 1) * BLOCK] = s
            top = jnp.max(s.reshape(BLOCK // 8, 8, width), axis=0)
            peak = top if peak is None else jnp.maximum(peak, top)
        peak = jnp.max(peak, axis=0, keepdims=True)
        acc = jnp.zeros((chans + AUG, width), F32)
        for j in range(0, MAX_KEYS, 2):
            e = jnp.exp2((s_ref[j * BLOCK : (j + 2) * BLOCK] - peak) * RAW)
            e_hi = e.astype(BF16)
            e_lo = (e - e_hi.astype(F32)).astype(BF16)
            v_pair = jnp.concatenate([vn_ref[slots[j]], vn_ref[slots[j + 1]]], axis=1)
            acc = acc + dot(v_pair, e_hi) + dot(v_pair, e_lo)
        whole = acc[chans : chans + 1]
        att_ref[:, lane_block(i)] = pick_heads(acc[:chans] * (1.0 / whole), heads)
        t_ref[pl.ds(i, 1), :] = peak + jnp.log2(whole) * (1.0 / RAW)
        return carry

    lax.fori_loop(0, blocks, body, 0)


def project_kernel(count, att_ref, w_ref, *refs):
    parts, (grad_ref, gw_ref) = refs[:count], refs[count:]
    depth = parts[0].shape[0]
    full = jnp.concatenate([p[...] for p in parts], axis=0)
    here = lax.axis_index("head") * depth
    wide = count * depth
    turned = pltpu.roll(w_ref[...].astype(F32), lax.rem(wide - here, wide), 1).astype(BF16)
    grad_ref[...] = dot(turned, full).astype(BF16)
    gw_ref[...] = pltpu.roll(dot_nt(att_ref[...].astype(BF16), full), here, 1)


def grads_kernel(
    lists_ref, counts_ref, q_ref, g_ref, att_ref, t_ref, ka_ref, va_ref, kn_ref,
    dq_ref, own_ref, lo_ref, hi_ref, acc_ref,
):
    chans = q_ref.shape[0]
    heads = chans // HEAD_DIM
    blocks = q_ref.shape[1] // BLOCK
    ext = blocks + 2 * RIM
    width = heads * BLOCK
    first_block = lax.axis_index("band") * blocks - RIM
    acc_ref[...] = jnp.zeros_like(acc_ref)
    pad_w = jnp.zeros((BLOCK - chans - AUG, width), BF16)
    none = jnp.zeros((chans, width), BF16)

    def body(i, carry):
        g_blk = g_ref[:, lane_block(i)]
        prod = g_blk.astype(F32) * att_ref[:, lane_block(i)]
        spread = jnp.concatenate(
            [
                jnp.sum(prod[h * HEAD_DIM : (h + 1) * HEAD_DIM], axis=0, keepdims=True)
                for h in range(heads)
            ],
            axis=1,
        )
        q_wide = spread_heads(q_ref[:, lane_block(i)], heads)
        g_wide = spread_heads(g_blk, heads)
        t_hi, t_mid, t_low = split3(-t_ref[pl.ds(i, 1), :])
        q_aug = jnp.concatenate(
            [q_wide, aug_rows([1.0, 1.0, 1.0, t_hi, t_mid, t_low], width), pad_w], axis=0
        )
        g_aug = jnp.concatenate([g_wide, aug_rows(split3(-spread), width), pad_w], axis=0)
        q_out = jnp.concatenate([q_wide, none], axis=0)
        g_out = jnp.concatenate([none, g_wide], axis=0)
        slots = [slot_of(lists_ref, counts_ref, i, j, first_block, ext) for j in range(MAX_KEYS)]
        dq = jnp.zeros((chans, width), F32)
        for j in range(0, MAX_KEYS, 2):
            lows = []
            for slot in slots[j : j + 2]:
                probs = jnp.exp2(dot(ka_ref[slot], q_aug) * RAW)
                dlow = (probs * dot(va_ref[slot], g_aug)).astype(BF16)
                acc_ref[slot] += dot_nt(probs.astype(BF16), g_out) + dot_nt(dlow, q_out)
                lows.append(dlow)
            k_pair = jnp.concatenate([kn_ref[slots[j]], kn_ref[slots[j + 1]]], axis=1)
            dq = dq + dot(k_pair, jnp.concatenate(lows, axis=0))
        dq_ref[:, lane_block(i)] = (pick_heads(dq, heads) * SCALE).astype(BF16)
        return carry

    lax.fori_loop(0, blocks, body, 0)
    lane = lax.broadcasted_iota(jnp.int32, (BLOCK, 2 * chans), 1)
    factor = jnp.where(lane < chans, SCALE, 1.0).astype(F32)
    for b in range(ext):
        x = acc_ref[b] * factor
        if b < RIM:
            lo_ref[b] = x.astype(BF16)
        elif b < RIM + blocks:
            own_ref[b - RIM] = x
        else:
            hi_ref[b - RIM - blocks] = x.astype(BF16)


def join_kernel(own_ref, below_ref, above_ref, dk_ref, dv_ref):
    blocks = own_ref.shape[0]
    chans = dk_ref.shape[0]
    for b in range(blocks):
        x = own_ref[b]
        if b < RIM:
            x = x + below_ref[b].astype(F32)
        if b >= blocks - RIM:
            x = x + above_ref[b - (blocks - RIM)].astype(F32)
        x = x.T
        dk_ref[:, b * BLOCK : (b + 1) * BLOCK] = x[:chans].astype(BF16)
        dv_ref[:, b * BLOCK : (b + 1) * BLOCK] = x[chans:].astype(BF16)


def kernel_call(body, outs, operands, scratch=(), smem=0, flops=0, transcendentals=0):
    size = sum(x.size * x.dtype.itemsize for x in operands + outs)
    vmem = pl.BlockSpec(memory_space=pltpu.VMEM)
    scalars = pl.BlockSpec(memory_space=pltpu.SMEM)
    return pl.pallas_call(
        body,
        out_shape=outs,
        in_specs=[scalars] * smem + [vmem] * (len(operands) - smem),
        out_specs=[vmem] * len(outs),
        scratch_shapes=list(scratch),
        compiler_params=pltpu.CompilerParams(vmem_limit_bytes=VMEM_LIMIT),
        cost_estimate=pl.CostEstimate(
            flops=flops, bytes_accessed=size, transcendentals=transcendentals
        ),
    )(*operands)


def moved(value, axis, steps):
    count = lax.axis_size(axis)
    return lax.ppermute(
        value, axis, [(i, i + steps) for i in range(count) if 0 <= i + steps < count]
    )


def sum_over(value, axis):
    count = lax.axis_size(axis)
    if count & (count - 1):
        return lax.psum(value, axis)
    step = 1
    while step < count:
        value = value + lax.ppermute(value, axis, [(i, i ^ step) for i in range(count)])
        step *= 2
    return value


def shards(queries, keys, values, grad_out, w_out, key_lists, key_counts):
    chans, tokens = queries.shape
    blocks = tokens // BLOCK
    heads = chans // HEAD_DIM
    ext = blocks + 2 * RIM
    width = heads * BLOCK
    total = tokens * lax.axis_size("band")
    head_count = lax.axis_size("head")
    rim = RIM * BLOCK
    shape = jax.ShapeDtypeStruct
    pairs = blocks * MAX_KEYS * width * BLOCK

    low = moved(jnp.stack([keys[:, -rim:], values[:, -rim:]]), "band", 1)
    high = moved(jnp.stack([keys[:, :rim], values[:, :rim]]), "band", -1)
    parts = [grad_out] + [
        lax.ppermute(grad_out, "head", [((i + s) % head_count, i) for i in range(head_count)])
        for s in range(1, head_count)
    ]
    ka, va, kn, att, t = kernel_call(
        functools.partial(attend_kernel, total),
        [
            shape((ext + 1, BLOCK, BLOCK), BF16),
            shape((ext + 1, BLOCK, BLOCK), BF16),
            shape((ext + 1, chans, BLOCK), BF16),
            shape((chans, tokens), F32),
            shape((blocks, width), F32),
        ],
        [key_lists, key_counts, queries, keys, values, low, high],
        [pltpu.VMEM((ext + 1, chans + AUG, BLOCK), BF16), pltpu.VMEM((MAX_KEYS * BLOCK, width), F32)],
        smem=2,
        flops=3 * 2 * pairs * BLOCK,
        transcendentals=pairs,
    )
    grad_att, part_w = kernel_call(
        functools.partial(project_kernel, head_count),
        [shape((chans, tokens), BF16), shape(w_out.shape, F32)],
        [att, w_out] + parts,
        flops=4 * w_out.size * tokens,
    )
    dq, own, lo, hi = kernel_call(
        grads_kernel,
        [
            shape((chans, tokens), BF16),
            shape((blocks, BLOCK, 2 * chans), F32),
            shape((RIM, BLOCK, 2 * chans), BF16),
            shape((RIM, BLOCK, 2 * chans), BF16),
        ],
        [key_lists, key_counts, queries, grad_att, att, t, ka, va, kn],
        [pltpu.VMEM((ext + 1, BLOCK, 2 * chans), F32)],
        smem=2,
        flops=5 * 2 * pairs * BLOCK,
        transcendentals=pairs,
    )
    above = moved(lo, "band", -1)
    below = moved(hi, "band", 1)
    grad_w = sum_over(part_w, "band")
    dk, dv = kernel_call(
        join_kernel,
        [shape((chans, tokens), BF16), shape((chans, tokens), BF16)],
        [own, below, above],
    )
    return (dq, dk, dv, grad_w)


def solution(mesh):
    in_specs = (
        P("head", "band"),
        P("head", "band"),
        P("head", "band"),
        P("head", "band"),
        P("head", None),
        P("band", None),
        P("band"),
    )
    out_specs = (P("head", "band"), P("head", "band"), P("head", "band"), P("head", None))
    return jax.shard_map(shards, mesh=mesh, in_specs=in_specs, out_specs=out_specs, check_vma=False)
```

```python
import functools

import jax
import jax.numpy as jnp
from jax import lax
from jax.experimental import pallas as pl
from jax.experimental.pallas import tpu as pltpu
from jax.sharding import PartitionSpec as P

HEAD_DIM = 32
BLOCK = 128
REACH = 4
MAX_KEYS = 8
RIM = 2 * REACH
SCALE = HEAD_DIM ** (-0.5)
LOG2E = 1.4426950408889634
RAW = SCALE * LOG2E
MASKED = -1e30
AUG = 16
F32 = jnp.float32
BF16 = jnp.bfloat16
VMEM_LIMIT = 48 * 1024 * 1024


def dot(a, b):
    return lax.dot_general(a, b, (((1,), (0,)), ((), ())), preferred_element_type=F32)


def dot_nt(a, b):
    return lax.dot_general(a, b, (((1,), (1,)), ((), ())), preferred_element_type=F32)


def split3(x):
    hi = x.astype(BF16).astype(F32)
    rest = x - hi
    mid = rest.astype(BF16).astype(F32)
    return hi, mid, (rest - mid).astype(BF16).astype(F32)


def aug_rows(rows, width):
    at = lax.broadcasted_iota(jnp.int32, (AUG, width), 0)
    out = jnp.zeros((AUG, width), F32)
    for i, row in enumerate(rows):
        out = jnp.where(at == i, row, out)
    return out.astype(BF16)


def spread_heads(x, heads):
    zero = jnp.zeros((HEAD_DIM, BLOCK), x.dtype)
    rows = []
    for h in range(heads):
        part = x[h * HEAD_DIM : (h + 1) * HEAD_DIM]
        rows.append(jnp.concatenate([part if g == h else zero for g in range(heads)], axis=1))
    return jnp.concatenate(rows, axis=0)


def pick_heads(x, heads):
    return jnp.concatenate(
        [
            x[h * HEAD_DIM : (h + 1) * HEAD_DIM, h * BLOCK : (h + 1) * BLOCK]
            for h in range(heads)
        ],
        axis=0,
    )


def slot_of(lists_ref, counts_ref, row, j, first_block, ext):
    return jnp.where(j < counts_ref[row], lists_ref[row, j] - first_block, ext)


def lane_block(i):
    return pl.ds(pl.multiple_of(i * BLOCK, BLOCK), BLOCK)


def attend_kernel(
    total, lists_ref, counts_ref, q_ref, k_ref, v_ref, lo_ref, hi_ref,
    ka_ref, va_ref, kn_ref, att_ref, t_ref, vn_ref, s_ref,
):
    chans = q_ref.shape[0]
    heads = chans // HEAD_DIM
    blocks = q_ref.shape[1] // BLOCK
    ext = blocks + 2 * RIM
    width = heads * BLOCK
    first_block = lax.axis_index("band") * blocks - RIM

    at = lax.broadcasted_iota(jnp.int32, (ext, BLOCK), 0) * BLOCK
    at = at + lax.broadcasted_iota(jnp.int32, (ext, BLOCK), 1) + first_block * BLOCK
    at = jnp.clip(at, 0, total - 1).astype(F32)
    logw = jnp.log(jnp.sin(jnp.pi * (at + 0.5) / total))
    hi, mid, low = split3(logw * (1.0 / SCALE))
    pad = jnp.zeros((BLOCK - chans - AUG, BLOCK), BF16)
    v_aug = aug_rows([1.0, 1.0, 1.0], BLOCK)
    for b in range(ext + 1):
        if b == ext:
            k_blk = jnp.zeros((chans, BLOCK), BF16)
            v_blk = k_blk
            k_aug = aug_rows([MASKED, 0.0, 0.0, 1.0, 1.0, 1.0], BLOCK)
        else:
            if b < RIM:
                at_lanes = slice(b * BLOCK, (b + 1) * BLOCK)
                k_blk, v_blk = lo_ref[0, :, at_lanes], lo_ref[1, :, at_lanes]
            elif b < RIM + blocks:
                at_lanes = slice((b - RIM) * BLOCK, (b - RIM + 1) * BLOCK)
                k_blk, v_blk = k_ref[:, at_lanes], v_ref[:, at_lanes]
            else:
                at_lanes = slice((b - RIM - blocks) * BLOCK, (b - RIM - blocks + 1) * BLOCK)
                k_blk, v_blk = hi_ref[0, :, at_lanes], hi_ref[1, :, at_lanes]
            k_aug = aug_rows(
                [hi[b : b + 1], mid[b : b + 1], low[b : b + 1], 1.0, 1.0, 1.0], BLOCK
            )
        kn_ref[b] = k_blk
        v_with = jnp.concatenate([v_blk, v_aug], axis=0)
        vn_ref[b] = v_with
        ka_ref[b] = jnp.concatenate([k_blk, k_aug, pad], axis=0).T
        va_ref[b] = jnp.concatenate([v_with, pad], axis=0).T

    ones = aug_rows([1.0, 1.0, 1.0], width)
    pad_w = jnp.zeros((BLOCK - chans - AUG, width), BF16)

    def body(i, carry):
        q_aug = jnp.concatenate([spread_heads(q_ref[:, lane_block(i)], heads), ones, pad_w], axis=0)
        slots = [slot_of(lists_ref, counts_ref, i, j, first_block, ext) for j in range(MAX_KEYS)]
        k_rows = jnp.concatenate([ka_ref[slot] for slot in slots], axis=0)
        s = dot(k_rows, q_aug)
        peak = jnp.max(jnp.max(s.reshape(-1, 8, width), axis=0), axis=0, keepdims=True)
        e = jnp.exp2((s - peak) * RAW)
        e_hi = e.astype(BF16)
        e_lo = (e - e_hi.astype(F32)).astype(BF16)
        v_cols = jnp.concatenate([vn_ref[slot] for slot in slots], axis=1)
        acc = dot(v_cols, e_hi) + dot(v_cols, e_lo)
        whole = acc[chans : chans + 1]
        att_ref[:, lane_block(i)] = pick_heads(acc[:chans] * (1.0 / whole), heads)
        t_ref[pl.ds(i, 1), :] = peak + jnp.log2(whole) * (1.0 / RAW)
        return carry

    lax.fori_loop(0, blocks, body, 0, unroll=8)


def project_kernel(count, att_ref, w_ref, *refs):
    parts, (grad_ref, gw_ref) = refs[:count], refs[count:]
    depth = parts[0].shape[0]
    full = jnp.concatenate([p[...] for p in parts], axis=0)
    here = lax.axis_index("head") * depth
    wide = count * depth
    turned = pltpu.roll(w_ref[...].astype(F32), lax.rem(wide - here, wide), 1).astype(BF16)
    grad_ref[...] = dot(turned, full).astype(BF16)
    gw_ref[...] = pltpu.roll(dot_nt(att_ref[...].astype(BF16), full), here, 1)


def grads_kernel(
    lists_ref, counts_ref, q_ref, g_ref, att_ref, t_ref, ka_ref, va_ref, kn_ref,
    dq_ref, own_ref, lo_ref, hi_ref, acc_ref,
):
    chans = q_ref.shape[0]
    heads = chans // HEAD_DIM
    blocks = q_ref.shape[1] // BLOCK
    ext = blocks + 2 * RIM
    width = heads * BLOCK
    first_block = lax.axis_index("band") * blocks - RIM
    acc_ref[...] = jnp.zeros_like(acc_ref)
    pad_w = jnp.zeros((BLOCK - chans - AUG, width), BF16)
    none = jnp.zeros((chans, width), BF16)

    def body(i, carry):
        g_blk = g_ref[:, lane_block(i)]
        prod = g_blk.astype(F32) * att_ref[:, lane_block(i)]
        spread = jnp.concatenate(
            [
                jnp.sum(prod[h * HEAD_DIM : (h + 1) * HEAD_DIM], axis=0, keepdims=True)
                for h in range(heads)
            ],
            axis=1,
        )
        q_wide = spread_heads(q_ref[:, lane_block(i)], heads)
        g_wide = spread_heads(g_blk, heads)
        t_hi, t_mid, t_low = split3(-t_ref[pl.ds(i, 1), :])
        q_aug = jnp.concatenate(
            [q_wide, aug_rows([1.0, 1.0, 1.0, t_hi, t_mid, t_low], width), pad_w], axis=0
        )
        g_aug = jnp.concatenate([g_wide, aug_rows(split3(-spread), width), pad_w], axis=0)
        q_out = jnp.concatenate([q_wide, none], axis=0)
        g_out = jnp.concatenate([none, g_wide], axis=0)
        slots = [slot_of(lists_ref, counts_ref, i, j, first_block, ext) for j in range(MAX_KEYS)]
        k_rows = jnp.concatenate([ka_ref[slot] for slot in slots], axis=0)
        v_rows = jnp.concatenate([va_ref[slot] for slot in slots], axis=0)
        probs = jnp.exp2(dot(k_rows, q_aug) * RAW)
        dlow = (probs * dot(v_rows, g_aug)).astype(BF16)
        both = dot_nt(probs.astype(BF16), g_out) + dot_nt(dlow, q_out)
        for j in range(MAX_KEYS):
            acc_ref[slots[j]] += both[j * BLOCK : (j + 1) * BLOCK]
        dq = dot(jnp.concatenate([kn_ref[slot] for slot in slots], axis=1), dlow)
        dq_ref[:, lane_block(i)] = (pick_heads(dq, heads) * SCALE).astype(BF16)
        return carry

    lax.fori_loop(0, blocks, body, 0, unroll=8)
    lane = lax.broadcasted_iota(jnp.int32, (BLOCK, 2 * chans), 1)
    factor = jnp.where(lane < chans, SCALE, 1.0).astype(F32)
    for b in range(ext):
        x = acc_ref[b] * factor
        if b < RIM:
            lo_ref[b] = x.astype(BF16)
        elif b < RIM + blocks:
            own_ref[b - RIM] = x
        else:
            hi_ref[b - RIM - blocks] = x.astype(BF16)


def join_kernel(own_ref, below_ref, above_ref, dk_ref, dv_ref):
    blocks = own_ref.shape[0]
    chans = dk_ref.shape[0]
    for b in range(blocks):
        x = own_ref[b]
        if b < RIM:
            x = x + below_ref[b].astype(F32)
        if b >= blocks - RIM:
            x = x + above_ref[b - (blocks - RIM)].astype(F32)
        x = x.T
        dk_ref[:, b * BLOCK : (b + 1) * BLOCK] = x[:chans].astype(BF16)
        dv_ref[:, b * BLOCK : (b + 1) * BLOCK] = x[chans:].astype(BF16)


def kernel_call(body, outs, operands, scratch=(), smem=0, flops=0, transcendentals=0):
    size = sum(x.size * x.dtype.itemsize for x in operands + outs)
    vmem = pl.BlockSpec(memory_space=pltpu.VMEM)
    scalars = pl.BlockSpec(memory_space=pltpu.SMEM)
    return pl.pallas_call(
        body,
        out_shape=outs,
        in_specs=[scalars] * smem + [vmem] * (len(operands) - smem),
        out_specs=[vmem] * len(outs),
        scratch_shapes=list(scratch),
        compiler_params=pltpu.CompilerParams(vmem_limit_bytes=VMEM_LIMIT),
        cost_estimate=pl.CostEstimate(
            flops=flops, bytes_accessed=size, transcendentals=transcendentals
        ),
    )(*operands)


def moved(value, axis, steps):
    count = lax.axis_size(axis)
    return lax.ppermute(
        value, axis, [(i, i + steps) for i in range(count) if 0 <= i + steps < count]
    )


def sum_over(value, axis):
    count = lax.axis_size(axis)
    if count & (count - 1):
        return lax.psum(value, axis)
    step = 1
    while step < count:
        value = value + lax.ppermute(value, axis, [(i, i ^ step) for i in range(count)])
        step *= 2
    return value


def shards(queries, keys, values, grad_out, w_out, key_lists, key_counts):
    chans, tokens = queries.shape
    blocks = tokens // BLOCK
    heads = chans // HEAD_DIM
    ext = blocks + 2 * RIM
    width = heads * BLOCK
    total = tokens * lax.axis_size("band")
    head_count = lax.axis_size("head")
    rim = RIM * BLOCK
    shape = jax.ShapeDtypeStruct
    pairs = blocks * MAX_KEYS * width * BLOCK

    low = moved(jnp.stack([keys[:, -rim:], values[:, -rim:]]), "band", 1)
    high = moved(jnp.stack([keys[:, :rim], values[:, :rim]]), "band", -1)
    parts = [grad_out] + [
        lax.ppermute(grad_out, "head", [((i + s) % head_count, i) for i in range(head_count)])
        for s in range(1, head_count)
    ]
    ka, va, kn, att, t = kernel_call(
        functools.partial(attend_kernel, total),
        [
            shape((ext + 1, BLOCK, BLOCK), BF16),
            shape((ext + 1, BLOCK, BLOCK), BF16),
            shape((ext + 1, chans, BLOCK), BF16),
            shape((chans, tokens), F32),
            shape((blocks, width), F32),
        ],
        [key_lists, key_counts, queries, keys, values, low, high],
        [pltpu.VMEM((ext + 1, chans + AUG, BLOCK), BF16), pltpu.VMEM((MAX_KEYS * BLOCK, width), F32)],
        smem=2,
        flops=3 * 2 * pairs * BLOCK,
        transcendentals=pairs,
    )
    grad_att, part_w = kernel_call(
        functools.partial(project_kernel, head_count),
        [shape((chans, tokens), BF16), shape(w_out.shape, F32)],
        [att, w_out] + parts,
        flops=4 * w_out.size * tokens,
    )
    dq, own, lo, hi = kernel_call(
        grads_kernel,
        [
            shape((chans, tokens), BF16),
            shape((blocks, BLOCK, 2 * chans), F32),
            shape((RIM, BLOCK, 2 * chans), BF16),
            shape((RIM, BLOCK, 2 * chans), BF16),
        ],
        [key_lists, key_counts, queries, grad_att, att, t, ka, va, kn],
        [pltpu.VMEM((ext + 1, BLOCK, 2 * chans), F32)],
        smem=2,
        flops=5 * 2 * pairs * BLOCK,
        transcendentals=pairs,
    )
    above = moved(lo, "band", -1)
    below = moved(hi, "band", 1)
    grad_w = sum_over(part_w, "band")
    dk, dv = kernel_call(
        join_kernel,
        [shape((chans, tokens), BF16), shape((chans, tokens), BF16)],
        [own, below, above],
    )
    return (dq, dk, dv, grad_w)


def solution(mesh):
    in_specs = (
        P("head", "band"),
        P("head", "band"),
        P("head", "band"),
        P("head", "band"),
        P("head", None),
        P("band", None),
        P("band"),
    )
    out_specs = (P("head", "band"), P("head", "band"), P("head", "band"), P("head", None))
    return jax.shard_map(shards, mesh=mesh, in_specs=in_specs, out_specs=out_specs, check_vma=False)
```

```python
import functools

import jax
import jax.numpy as jnp
from jax import lax
from jax.experimental import pallas as pl
from jax.experimental.pallas import tpu as pltpu
from jax.sharding import PartitionSpec as P

HEAD_DIM = 32
BLOCK = 128
REACH = 4
MAX_KEYS = 8
RIM = 2 * REACH
SCALE = HEAD_DIM ** (-0.5)
LOG2E = 1.4426950408889634
RAW = SCALE * LOG2E
MASKED = -1e30
AUG = 16
F32 = jnp.float32
BF16 = jnp.bfloat16
VMEM_LIMIT = 48 * 1024 * 1024


def dot(a, b):
    return lax.dot_general(a, b, (((1,), (0,)), ((), ())), preferred_element_type=F32)


def dot_nt(a, b):
    return lax.dot_general(a, b, (((1,), (1,)), ((), ())), preferred_element_type=F32)


def split3(x):
    hi = x.astype(BF16).astype(F32)
    rest = x - hi
    mid = rest.astype(BF16).astype(F32)
    return hi, mid, (rest - mid).astype(BF16).astype(F32)


def aug_rows(rows, width):
    at = lax.broadcasted_iota(jnp.int32, (AUG, width), 0)
    out = jnp.zeros((AUG, width), F32)
    for i, row in rows.items():
        out = jnp.where(at == i, row, out)
    return out.astype(BF16)


ROW_BIAS, ROW_LSE, ROW_SPREAD, ROW_UP, ROW_DOWN = 0, 3, 8, 12, 13


def three(first, rows):
    return {first + i: row for i, row in enumerate(rows)}


ONES = (1.0, 1.0, 1.0)


def spread_heads(x, heads):
    zero = jnp.zeros((HEAD_DIM, BLOCK), x.dtype)
    rows = []
    for h in range(heads):
        part = x[h * HEAD_DIM : (h + 1) * HEAD_DIM]
        rows.append(jnp.concatenate([part if g == h else zero for g in range(heads)], axis=1))
    return jnp.concatenate(rows, axis=0)


def pick_heads(x, heads):
    return jnp.concatenate(
        [
            x[h * HEAD_DIM : (h + 1) * HEAD_DIM, h * BLOCK : (h + 1) * BLOCK]
            for h in range(heads)
        ],
        axis=0,
    )


def lane_block(i):
    return slice(i * BLOCK, (i + 1) * BLOCK)


def start_copies(srcs, dsts, sems):
    copies = [pltpu.make_async_copy(s, d, sems.at[i]) for i, (s, d) in enumerate(zip(srcs, dsts))]
    for copy in copies:
        copy.start()
    return copies


def rim_bases(blocks):
    odd = lax.rem(lax.axis_index("band"), 2) == 1
    low, high = 0, RIM + blocks
    return jnp.where(odd, low, high), jnp.where(odd, high, low)


def rim_bases(blocks):
    odd = lax.rem(lax.axis_index("band"), 2) == 1
    low, high = 0, RIM + blocks
    return jnp.where(odd, low, high), jnp.where(odd, high, low)


def in_order(steps, begin, finish, ahead):
    begun = []
    for n, step in enumerate(steps):
        while len(begun) <= ahead and n + len(begun) < len(steps):
            begun.append(begin(steps[n + len(begun)]))
        finish(step, *begun.pop(0))


def place(refs, b, k_blk, v_blk, bias):
    ka_ref, va_ref, kn_ref, vn_ref = refs
    pad = jnp.zeros((BLOCK - k_blk.shape[0] - AUG, BLOCK), BF16)
    k_aug = aug_rows(three(ROW_BIAS, bias) | three(ROW_LSE, ONES), BLOCK)
    v_with = jnp.concatenate([v_blk, aug_rows(three(ROW_SPREAD, ONES), BLOCK)], axis=0)
    kn_ref[b] = k_blk
    vn_ref[b] = v_with
    ka_ref[b] = jnp.concatenate([k_blk, k_aug, pad], axis=0).T
    va_ref[b] = jnp.concatenate([v_with, pad], axis=0).T


def add_kernel(a_ref, b_ref, out_ref):
    out_ref[...] = a_ref[...] + b_ref[...]


def packed(chosen, values):
    shape = values.shape
    lane = lax.broadcasted_iota(jnp.int32, shape, 1)
    before = (
        lax.broadcasted_iota(jnp.int32, (BLOCK, BLOCK), 0)
        < lax.broadcasted_iota(jnp.int32, (BLOCK, BLOCK), 1)
    )
    rank = dot(chosen.astype(F32), before.astype(F32))
    out = jnp.zeros(shape, F32)
    for r in range(MAX_KEYS):
        hit = jnp.logical_and(chosen, rank == r)
        value = jnp.sum(jnp.where(hit, values.astype(F32) + 1.0, 0.0), axis=1, keepdims=True)
        out = jnp.where(lane == r, value, out)
    return out


def prepare_kernel(
    total, own_ref, lists_ref, counts_ref,
    slots_ref, carry_ref, bias_ref, ka_ref, va_ref, kn_ref, vn_ref,
    wide_ref, counts_smem, sems,
):
    copies = start_copies((counts_ref,), (counts_smem,), sems)
    chans = own_ref.shape[1]
    blocks = own_ref.shape[2] // BLOCK
    ext = blocks + 2 * RIM
    first_block = lax.axis_index("band") * blocks - RIM
    at = lax.broadcasted_iota(jnp.int32, (ext, BLOCK), 0) * BLOCK
    at = at + lax.broadcasted_iota(jnp.int32, (ext, BLOCK), 1) + first_block * BLOCK
    at = jnp.clip(at, 0, total - 1).astype(F32)
    logw = jnp.log(jnp.sin(jnp.pi * (at + 0.5) / total))
    bias = split3(logw * (1.0 / SCALE))
    for i, part in enumerate(bias):
        bias_ref[i] = part
    refs = (ka_ref, va_ref, kn_ref, vn_ref)
    none = jnp.zeros((chans, BLOCK), BF16)
    place(refs, ext, none, none, [MASKED, 0.0, 0.0])
    for b in range(blocks):
        rows = [part[RIM + b : RIM + b + 1] for part in bias]
        place(refs, RIM + b, own_ref[0, :, lane_block(b)], own_ref[1, :, lane_block(b)], rows)
    for copy in copies:
        copy.wait()
    wide_ref[...] = jnp.zeros_like(wide_ref)
    wide_ref[:, :MAX_KEYS] = lists_ref[...]
    lane = lax.broadcasted_iota(jnp.int32, (blocks, BLOCK), 1)
    row = lax.broadcasted_iota(jnp.int32, (blocks, BLOCK), 0)
    used = jnp.zeros((blocks, BLOCK), jnp.int32)
    for i in range(blocks):
        used = jnp.where(row == i, counts_smem[i], used)
    slots = jnp.where(lane < used, wide_ref[...] - first_block, ext)
    slots_ref[...] = slots
    upper = RIM + blocks
    carry_ref[0] = packed(jnp.logical_and(slots >= upper, slots < ext), slots - upper)
    carry_ref[1] = packed(slots < RIM, slots)


def attend_kernel(
    slots_vmem, own_ref, bias_ref, pair_ref, other_ref, ka_in, va_in, kn_in, vn_in,
    ka_ref, va_ref, kn_ref, vn_ref, att_ref, t_ref, slots_ref, sems,
):
    copies = start_copies((slots_vmem,), (slots_ref,), sems)
    chans = own_ref.shape[1]
    heads = chans // HEAD_DIM
    blocks = own_ref.shape[2] // BLOCK
    width = heads * BLOCK
    refs = (ka_ref, va_ref, kn_ref, vn_ref)
    for base, ref in zip(rim_bases(blocks), (pair_ref, other_ref)):
        for b in range(RIM):
            rows = [bias_ref[i, pl.ds(base + b, 1), :] for i in range(3)]
            place(refs, base + b, ref[0, :, lane_block(b)], ref[1, :, lane_block(b)], rows)
    for copy in copies:
        copy.wait()

    ones = aug_rows(three(ROW_BIAS, ONES), width)
    pad_w = jnp.zeros((BLOCK - chans - AUG, width), BF16)

    def scores(i):
        q_aug = jnp.concatenate([spread_heads(own_ref[2, :, lane_block(i)], heads), ones, pad_w], axis=0)
        slots = [slots_ref[i, j] for j in range(MAX_KEYS)]
        k_rows = jnp.concatenate([ka_ref[slot] for slot in slots], axis=0)
        s = dot(k_rows, q_aug)
        peak = jnp.max(jnp.max(s.reshape(-1, 8, width), axis=0), axis=0, keepdims=True)
        return slots, s, peak

    def finish(i, slots, s, peak):
        e = jnp.exp2((s - peak) * RAW)
        v_cols = jnp.concatenate([vn_ref[slot] for slot in slots], axis=1)
        acc = dot(v_cols, e.astype(BF16))
        whole = acc[chans + ROW_SPREAD : chans + ROW_SPREAD + 1]
        att_ref[:, lane_block(i)] = pick_heads(acc[:chans] * (1.0 / whole), heads)
        t_ref[i : i + 1] = peak + jnp.log2(whole) * (1.0 / RAW)

    in_order(range(blocks), scores, finish, 2)


def reorder(x, count):
    depth = x.shape[1] // count
    here = lax.axis_index("head")
    bit = 1
    while bit < count:
        parts = [x[:, (m ^ bit) * depth : ((m ^ bit) + 1) * depth] for m in range(count)]
        x = jnp.where((here & bit) != 0, jnp.concatenate(parts, axis=1), x)
        bit *= 2
    return x


def project_kernel(count, att_ref, t_ref, carry_ref, w_ref, *refs):
    parts, (z_ref, gw_ref) = refs[:count], refs[count:]
    chans, tokens = att_ref.shape
    full = jnp.concatenate([p[...] for p in parts], axis=0)
    turned = reorder(w_ref[...].astype(F32), count).astype(BF16)
    grad = dot(turned, full).astype(BF16)
    z_ref[:chans] = grad
    prod = grad.astype(F32) * att_ref[...]
    for h in range(chans // HEAD_DIM):
        spread = jnp.sum(prod[h * HEAD_DIM : (h + 1) * HEAD_DIM], axis=0, keepdims=True)
        first = chans + h * AUG
        for i in range(tokens // BLOCK):
            t = t_ref[i : i + 1, h * BLOCK : (h + 1) * BLOCK]
            rows = three(ROW_BIAS, ONES) | three(ROW_LSE, split3(-t))
            rows |= three(ROW_SPREAD, split3(-spread[:, lane_block(i)]))
            rows |= {ROW_UP: carry_ref[0, i : i + 1, :], ROW_DOWN: carry_ref[1, i : i + 1, :]}
            z_ref[first : first + AUG, lane_block(i)] = aug_rows(rows, BLOCK)
    gw_ref[...] = reorder(dot_nt(att_ref[...].astype(BF16), full), count)


def query_side(q_ref, z_ref, here):
    chans = q_ref.shape[0]
    heads = chans // HEAD_DIM
    width = heads * BLOCK
    q_wide = spread_heads(q_ref[:, here], heads)
    g_wide = spread_heads(z_ref[:chans, here], heads)
    tiles = [z_ref[chans + h * AUG : chans + (h + 1) * AUG, here] for h in range(heads)]
    aug = jnp.concatenate(tiles, axis=1)
    pad = jnp.zeros((BLOCK - chans - AUG, width), BF16)
    none = jnp.zeros((chans, width), BF16)
    q_aug = jnp.concatenate([q_wide, aug, pad], axis=0)
    g_aug = jnp.concatenate([g_wide, aug, pad], axis=0)
    q_out = jnp.concatenate([q_wide, none], axis=0)
    g_out = jnp.concatenate([none, g_wide], axis=0)
    return q_aug, g_aug, q_out, g_out


def products(side, slots, ka_ref, va_ref):
    q_aug, g_aug = side[:2]
    k_rows = jnp.concatenate([ka_ref[slot] for slot in slots], axis=0)
    v_rows = jnp.concatenate([va_ref[slot] for slot in slots], axis=0)
    return dot(k_rows, q_aug), dot(v_rows, g_aug)


def pair_grads(side, slots, scores, dprobs, acc_ref):
    q_out, g_out = side[2:]
    probs = jnp.exp2(scores * RAW)
    dlow = (probs * dprobs).astype(BF16)
    both = dot_nt(probs.astype(BF16), g_out) + dot_nt(dlow, q_out)
    for j, slot in enumerate(slots):
        acc_ref[slot] += both[j * BLOCK : (j + 1) * BLOCK]
    return dlow


def grads_kernel(start, stop, slots_vmem, own_ref, z_ref, ka_ref, va_ref, kn_ref, *refs):
    dq_ref, acc_ref, slots_ref, sems = refs[-4:]
    copies = start_copies((slots_vmem,), (slots_ref,), sems)
    chans = dq_ref.shape[0]
    heads = chans // HEAD_DIM
    if start == 0:
        acc_ref[...] = jnp.zeros_like(acc_ref)
    for copy in copies:
        copy.wait()
    def begin(i):
        slots = [slots_ref[i, j] for j in range(MAX_KEYS)]
        side = query_side(own_ref.at[2], z_ref, lane_block(i))
        return side, slots, *products(side, slots, ka_ref, va_ref)

    def finish(i, side, slots, scores, dprobs):
        dlow = pair_grads(side, slots, scores, dprobs, acc_ref)
        dq = dot(jnp.concatenate([kn_ref[slot] for slot in slots], axis=1), dlow)
        dq_ref[:, lane_block(i - start)] = (pick_heads(dq, heads) * SCALE).astype(BF16)

    in_order(range(start, stop), begin, finish, 1)


def neighbours_kernel(
    dq_low, dq_high, past_ref, pair_own, other_own, pair_ref, other_ref, ka_ref, va_ref,
    dq_ref, dk_ref, dv_ref, acc_ref, q_all, z_all, lists_vmem, todo_ref, lists_ref, sems,
):
    chans = dk_ref.shape[0]
    blocks = dk_ref.shape[1] // BLOCK
    ext = blocks + 2 * RIM
    odd = lax.rem(lax.axis_index("band"), 2) == 1
    for s, (ref, below) in enumerate(((pair_ref, odd), (other_ref, jnp.logical_not(odd)))):
        rows = ref[chans : chans + AUG].astype(F32)
        row = jnp.where(below, rows[ROW_UP : ROW_UP + 1], rows[ROW_DOWN : ROW_DOWN + 1])
        for i in range(blocks):
            at = s * blocks + i
            lists_vmem[at : at + 1] = row[:, lane_block(i)].astype(jnp.int32)
    lists_vmem[2 * blocks :] = jnp.zeros_like(lists_vmem[2 * blocks :])
    copies = start_copies((lists_vmem,), (lists_ref,), sems)
    q_all[0] = pair_own[2]
    q_all[1] = other_own[2]
    z_all[0] = pair_ref[...]
    z_all[1] = other_ref[...]
    half = dq_low.shape[1]
    dq_ref[:, :half] = dq_low[...]
    dq_ref[:, half:] = dq_high[...]
    for b in range(blocks):
        acc_ref[RIM + b] = past_ref[RIM + b]
    acc_ref[ext] = past_ref[ext]
    for copy in copies:
        copy.wait()
    step, many = 2, 3
    count = 0
    for row in range(2 * blocks):
        for c in range(0, MAX_KEYS, step):
            todo_ref[count] = row * MAX_KEYS + c
            count = count + (lists_ref[row, c] > 0).astype(jnp.int32)
    for j in range(many):
        todo_ref[count + j] = 2 * blocks * MAX_KEYS

    def body(k, carry):
        begun = []
        for j in range(many):
            todo = todo_ref[k * many + j]
            row, c = todo // MAX_KEYS, todo % MAX_KEYS
            here = pl.ds(pl.multiple_of(row % blocks * BLOCK, BLOCK), BLOCK)
            at = jnp.minimum(row // blocks, 1)
            side = query_side(q_all.at[at], z_all.at[at], here)
            slots = []
            for n in range(step):
                place_of = lists_ref[row, c + n]
                slots.append(jnp.where(place_of > 0, RIM - 1 + place_of, ext))
            begun.append((side, slots, *products(side, slots, ka_ref, va_ref)))
        for one in begun:
            pair_grads(*one, acc_ref)
        return carry

    lax.fori_loop(0, (count + many - 1) // many, body, 0)
    factor = part_factor(2 * chans)
    for b in range(blocks):
        x = (acc_ref[RIM + b] * factor).T
        dk_ref[:, lane_block(b)] = x[:chans].astype(BF16)
        dv_ref[:, lane_block(b)] = x[chans:].astype(BF16)


def part_factor(lanes):
    lane = lax.broadcasted_iota(jnp.int32, (BLOCK, lanes), 1)
    return jnp.where(lane < lanes // 2, SCALE, 1.0).astype(F32)


def kernel_call(body, outs, operands, scalars=(), scratch=(), flops=0, transcendentals=0, aliases=None):
    size = sum(x.size * x.dtype.itemsize for x in operands + outs)
    vmem = pl.BlockSpec(memory_space=pltpu.VMEM)
    copies = [pltpu.SMEM(x.shape, x.dtype) for x in scalars]
    if copies:
        copies.append(pltpu.SemaphoreType.DMA((len(copies),)))
    return pl.pallas_call(
        body,
        out_shape=outs,
        in_specs=[vmem] * len(operands),
        out_specs=[vmem] * len(outs),
        scratch_shapes=list(scratch) + copies,
        input_output_aliases=aliases or {},
        compiler_params=pltpu.CompilerParams(vmem_limit_bytes=VMEM_LIMIT),
        cost_estimate=pl.CostEstimate(
            flops=flops, bytes_accessed=size, transcendentals=transcendentals
        ),
    )(*operands)


def to_pair(value, axis):
    last = lax.axis_size(axis) - 1
    return lax.ppermute(value, axis, [(i, i ^ 1) for i in range(last + 1) if i ^ 1 <= last])


def to_other(value, axis):
    last = lax.axis_size(axis) - 1
    swap = [(i, ((i + 1) ^ 1) - 1) for i in range(last + 1)]
    return lax.ppermute(value, axis, [(i, j) for i, j in swap if 0 <= j <= last])


def gathered(value, axis):
    count = lax.axis_size(axis)
    if count & (count - 1):
        raise ValueError("axis size")
    step, parts = count // 2, {0: value}
    while step:
        swap = [(i, i ^ step) for i in range(count)]
        parts.update({m ^ step: lax.ppermute(x, axis, swap) for m, x in list(parts.items())})
        step //= 2
    return [parts[m] for m in range(count)]


class sum_steps:
    def __init__(self, value, axis):
        self.axis, self.count, self.value = axis, lax.axis_size(axis), value
        if self.count & (self.count - 1):
            raise ValueError("axis size")
        sizes = [1 << i for i in range(self.count.bit_length() - 1)]
        self.steps = sizes[:1] + sizes[:0:-1]
        self.send()

    def send(self):
        step = self.steps.pop(0)
        swap = [(i, i ^ step) for i in range(self.count)]
        self.came = lax.ppermute(self.value, self.axis, swap)

    def add(self):
        shape = jax.ShapeDtypeStruct(self.value.shape, self.value.dtype)
        (self.value,) = kernel_call(add_kernel, [shape], [self.value, self.came])

    def go_on(self):
        self.add()
        self.send()


def shards(queries, keys, values, grad_out, w_out, key_lists, key_counts):
    chans, tokens = queries.shape
    blocks = tokens // BLOCK
    heads = chans // HEAD_DIM
    ext = blocks + 2 * RIM
    width = heads * BLOCK
    total = tokens * lax.axis_size("band")
    head_count = lax.axis_size("head")
    shape = jax.ShapeDtypeStruct
    pairs = blocks * MAX_KEYS * width * BLOCK

    if blocks != RIM:
        raise ValueError("band size")
    like = lambda x: shape(x.shape, x.dtype)
    own = jnp.stack([keys, values, queries])
    other_own = to_other(own, "band")
    pair_own = to_pair(own, "band")
    parts = gathered(grad_out, "head")
    slots, carry, bias, *state = kernel_call(
        functools.partial(prepare_kernel, total),
        [
            shape((blocks, BLOCK), jnp.int32),
            shape((2, blocks, BLOCK), F32),
            shape((3, ext, BLOCK), F32),
            shape((ext + 1, BLOCK, BLOCK), BF16),
            shape((ext + 1, BLOCK, BLOCK), BF16),
            shape((ext + 1, chans, BLOCK), BF16),
            shape((ext + 1, chans + AUG, BLOCK), BF16),
        ],
        [own, key_lists, key_counts],
        [key_counts],
        scratch=[pltpu.VMEM((blocks, BLOCK), jnp.int32)],
    )
    ka, va, kn, vn, att, t = kernel_call(
        attend_kernel,
        [like(x) for x in state] + [shape((chans, tokens), F32), shape((blocks, width), F32)],
        [slots, own, bias, pair_own, other_own] + state,
        [slots],
        flops=3 * 2 * pairs * BLOCK,
        transcendentals=pairs,
        aliases={5 + i: i for i in range(4)},
    )
    z, part_w = kernel_call(
        functools.partial(project_kernel, head_count),
        [shape((chans + heads * AUG, tokens), BF16), shape(w_out.shape, F32)],
        [att, t, carry, w_out] + parts,
        flops=4 * w_out.size * tokens,
    )
    other = to_other(z, "band")
    pair = to_pair(z, "band")
    sums = sum_steps(part_w, "band")
    acc = shape((ext + 1, BLOCK, 2 * chans), F32)
    common, state, dq_parts = [slots, own, z, ka, va, kn], [], []
    cuts = [0, blocks // 2, blocks]
    for start, stop in zip(cuts, cuts[1:]):
        dq, done = kernel_call(
            functools.partial(grads_kernel, start, stop),
            [shape((chans, (stop - start) * BLOCK), BF16), acc],
            common + state,
            [slots],
            flops=10 * pairs * BLOCK * (stop - start) // blocks,
            transcendentals=pairs * (stop - start) // blocks,
            aliases={len(common): 1} if state else None,
        )
        dq_parts.append(dq)
        done, sums.came = lax.optimization_barrier((done, sums.came))
        if sums.steps:
            sums.go_on()
            done, sums.value = lax.optimization_barrier((done, sums.value))
        state = [done]
    dq, dk, dv = kernel_call(
        neighbours_kernel,
        [shape((chans, tokens), BF16)] * 3,
        dq_parts + state + [pair_own, other_own, pair, other, ka, va],
        scratch=[
            pltpu.VMEM(acc.shape, F32),
            pltpu.VMEM((2,) + queries.shape, BF16),
            pltpu.VMEM((2,) + z.shape, BF16),
            pltpu.VMEM((2 * blocks + 8, BLOCK), jnp.int32),
            pltpu.SMEM((2 * blocks * MAX_KEYS + 8,), jnp.int32),
            pltpu.SMEM((2 * blocks + 8, BLOCK), jnp.int32),
            pltpu.SemaphoreType.DMA((1,)),
        ],
        flops=4 * pairs * BLOCK,
        transcendentals=pairs // 2,
    )
    dk, sums.came = lax.optimization_barrier((dk, sums.came))
    while sums.steps:
        sums.go_on()
    sums.add()
    return (dq, dk, dv, sums.value)


def solution(mesh):
    in_specs = (
        P("head", "band"),
        P("head", "band"),
        P("head", "band"),
        P("head", "band"),
        P("head", None),
        P("band", None),
        P("band"),
    )
    out_specs = (P("head", "band"), P("head", "band"), P("head", "band"), P("head", None))
    return jax.shard_map(shards, mesh=mesh, in_specs=in_specs, out_specs=out_specs, check_vma=False)
```

```python
import functools

import jax
import jax.numpy as jnp
from jax import lax
from jax.experimental import pallas as pl
from jax.experimental.pallas import tpu as pltpu
from jax.sharding import PartitionSpec as P

HEAD_DIM = 32
BLOCK = 128
REACH = 4
MAX_KEYS = 8
RIM = 2 * REACH
SCALE = HEAD_DIM ** (-0.5)
LOG2E = 1.4426950408889634
RAW = SCALE * LOG2E
MASKED = -1e30
AUG = 16
SIZES = (4, 6, MAX_KEYS)
EARLY = (4, 4, 4)
F32 = jnp.float32
BF16 = jnp.bfloat16
VMEM_LIMIT = 48 * 1024 * 1024


def dot(a, b):
    return lax.dot_general(a, b, (((1,), (0,)), ((), ())), preferred_element_type=F32)


def dot_nt(a, b):
    return lax.dot_general(a, b, (((1,), (1,)), ((), ())), preferred_element_type=F32)


def split3(x):
    hi = x.astype(BF16).astype(F32)
    rest = x - hi
    mid = rest.astype(BF16).astype(F32)
    return hi, mid, (rest - mid).astype(BF16).astype(F32)


def aug_rows(rows, width):
    at = lax.broadcasted_iota(jnp.int32, (AUG, width), 0)
    out = jnp.zeros((AUG, width), F32)
    for i, row in rows.items():
        out = jnp.where(at == i, row, out)
    return out.astype(BF16)


ROW_BIAS, ROW_LSE, ROW_SPREAD, ROW_UP, ROW_DOWN = 0, 3, 8, 12, 13


def three(first, rows):
    return {first + i: row for i, row in enumerate(rows)}


ONES = (1.0, 1.0, 1.0)


def spread_heads(x, heads):
    zero = jnp.zeros((HEAD_DIM, BLOCK), x.dtype)
    rows = []
    for h in range(heads):
        part = x[h * HEAD_DIM : (h + 1) * HEAD_DIM]
        rows.append(jnp.concatenate([part if g == h else zero for g in range(heads)], axis=1))
    return jnp.concatenate(rows, axis=0)


def pick_heads(x, heads):
    return jnp.concatenate(
        [
            x[h * HEAD_DIM : (h + 1) * HEAD_DIM, h * BLOCK : (h + 1) * BLOCK]
            for h in range(heads)
        ],
        axis=0,
    )


def lane_block(i):
    return slice(i * BLOCK, (i + 1) * BLOCK)


def start_copies(srcs, dsts, sems):
    copies = [pltpu.make_async_copy(s, d, sems.at[i]) for i, (s, d) in enumerate(zip(srcs, dsts))]
    for copy in copies:
        copy.start()
    return copies


def rim_bases(blocks):
    odd = lax.rem(lax.axis_index("band"), 2) == 1
    low, high = 0, RIM + blocks
    return jnp.where(odd, low, high), jnp.where(odd, high, low)


def rim_bases(blocks):
    odd = lax.rem(lax.axis_index("band"), 2) == 1
    low, high = 0, RIM + blocks
    return jnp.where(odd, low, high), jnp.where(odd, high, low)


def in_order(steps, begin, finish, ahead):
    begun = []
    for n, step in enumerate(steps):
        while len(begun) <= ahead and n + len(begun) < len(steps):
            begun.append(begin(steps[n + len(begun)]))
        finish(step, *begun.pop(0))


def place(refs, b, k_blk, v_blk, bias):
    ka_ref, va_ref, kn_ref, vn_ref = refs
    pad = jnp.zeros((BLOCK - k_blk.shape[0] - AUG, BLOCK), BF16)
    k_aug = aug_rows(three(ROW_BIAS, bias) | three(ROW_LSE, ONES), BLOCK)
    v_with = jnp.concatenate([v_blk, aug_rows(three(ROW_SPREAD, ONES), BLOCK)], axis=0)
    kn_ref[b] = k_blk
    vn_ref[b] = v_with
    ka_ref[b] = jnp.concatenate([k_blk, k_aug, pad], axis=0).T
    va_ref[b] = jnp.concatenate([v_with, pad], axis=0).T


def by_need(slots_ref, run):
    most = slots_ref[0, MAX_KEYS]
    for low, high in zip((0,) + SIZES, SIZES):
        pl.when(jnp.logical_and(most > low, most <= high))(functools.partial(run, high))


def add_kernel(a_ref, b_ref, out_ref):
    out_ref[...] = a_ref[...] + b_ref[...]


def packed(chosen, values):
    shape = values.shape
    lane = lax.broadcasted_iota(jnp.int32, shape, 1)
    before = (
        lax.broadcasted_iota(jnp.int32, (BLOCK, BLOCK), 0)
        < lax.broadcasted_iota(jnp.int32, (BLOCK, BLOCK), 1)
    )
    rank = dot(chosen.astype(F32), before.astype(F32))
    out = jnp.zeros(shape, F32)
    for r in range(MAX_KEYS):
        hit = jnp.logical_and(chosen, rank == r)
        value = jnp.sum(jnp.where(hit, values.astype(F32) + 1.0, 0.0), axis=1, keepdims=True)
        out = jnp.where(lane == r, value, out)
    return out


def prepare_kernel(
    total, own_ref, lists_ref, counts_ref,
    slots_ref, carry_ref, bias_ref, ka_ref, va_ref, kn_ref, vn_ref,
    wide_ref, counts_smem, sems,
):
    copies = start_copies((counts_ref,), (counts_smem,), sems)
    chans = own_ref.shape[1]
    blocks = own_ref.shape[2] // BLOCK
    ext = blocks + 2 * RIM
    first_block = lax.axis_index("band") * blocks - RIM
    at = lax.broadcasted_iota(jnp.int32, (ext, BLOCK), 0) * BLOCK
    at = at + lax.broadcasted_iota(jnp.int32, (ext, BLOCK), 1) + first_block * BLOCK
    at = jnp.clip(at, 0, total - 1).astype(F32)
    logw = jnp.log(jnp.sin(jnp.pi * (at + 0.5) / total))
    bias = split3(logw * (1.0 / SCALE))
    for i, part in enumerate(bias):
        bias_ref[i] = part
    refs = (ka_ref, va_ref, kn_ref, vn_ref)
    none = jnp.zeros((chans, BLOCK), BF16)
    place(refs, ext, none, none, [MASKED, 0.0, 0.0])
    for b in range(blocks):
        rows = [part[RIM + b : RIM + b + 1] for part in bias]
        place(refs, RIM + b, own_ref[0, :, lane_block(b)], own_ref[1, :, lane_block(b)], rows)
    for copy in copies:
        copy.wait()
    wide_ref[...] = jnp.zeros_like(wide_ref)
    wide_ref[:, :MAX_KEYS] = lists_ref[...]
    lane = lax.broadcasted_iota(jnp.int32, (blocks, BLOCK), 1)
    row = lax.broadcasted_iota(jnp.int32, (blocks, BLOCK), 0)
    used, most = jnp.zeros((blocks, BLOCK), jnp.int32), 0
    for i in range(blocks):
        used = jnp.where(row == i, counts_smem[i], used)
        most = jnp.maximum(most, counts_smem[i])
    slots = jnp.where(lane < used, wide_ref[...] - first_block, ext)
    slots_ref[...] = jnp.where(lane == MAX_KEYS, most, slots)
    upper = RIM + blocks
    carry_ref[0] = packed(jnp.logical_and(slots >= upper, slots < ext), slots - upper)
    carry_ref[1] = packed(slots < RIM, slots)


def attend_kernel(
    slots_vmem, own_ref, bias_ref, pair_ref, other_ref, ka_in, va_in, kn_in, vn_in,
    ka_ref, va_ref, kn_ref, vn_ref, att_ref, t_ref, slots_ref, sems,
):
    copies = start_copies((slots_vmem,), (slots_ref,), sems)
    chans = own_ref.shape[1]
    heads = chans // HEAD_DIM
    blocks = own_ref.shape[2] // BLOCK
    width = heads * BLOCK
    refs = (ka_ref, va_ref, kn_ref, vn_ref)
    for base, ref in zip(rim_bases(blocks), (pair_ref, other_ref)):
        for b in range(RIM):
            rows = [bias_ref[i, pl.ds(base + b, 1), :] for i in range(3)]
            place(refs, base + b, ref[0, :, lane_block(b)], ref[1, :, lane_block(b)], rows)
    for copy in copies:
        copy.wait()

    ones = aug_rows(three(ROW_BIAS, ONES), width)
    pad_w = jnp.zeros((BLOCK - chans - AUG, width), BF16)

    def scores(i):
        q_aug = jnp.concatenate([spread_heads(own_ref[2, :, lane_block(i)], heads), ones, pad_w], axis=0)
        slots = [slots_ref[i, j] for j in range(MAX_KEYS)]
        k_rows = jnp.concatenate([ka_ref[slot] for slot in slots], axis=0)
        s = dot(k_rows, q_aug)
        peak = jnp.max(jnp.max(s.reshape(-1, 8, width), axis=0), axis=0, keepdims=True)
        return slots, s, peak

    def finish(i, slots, s, peak):
        e = jnp.exp2((s - peak) * RAW)
        v_cols = jnp.concatenate([vn_ref[slot] for slot in slots], axis=1)
        acc = dot(v_cols, e.astype(BF16))
        whole = acc[chans + ROW_SPREAD : chans + ROW_SPREAD + 1]
        att_ref[:, lane_block(i)] = pick_heads(acc[:chans] * (1.0 / whole), heads)
        t_ref[i : i + 1] = peak + jnp.log2(whole) * (1.0 / RAW)

    in_order(range(blocks), scores, finish, 2)


def reorder(x, count):
    depth = x.shape[1] // count
    here = lax.axis_index("head")
    bit = 1
    while bit < count:
        parts = [x[:, (m ^ bit) * depth : ((m ^ bit) + 1) * depth] for m in range(count)]
        x = jnp.where((here & bit) != 0, jnp.concatenate(parts, axis=1), x)
        bit *= 2
    return x


def project_kernel(count, att_ref, t_ref, carry_ref, w_ref, *refs):
    parts, (z_ref, both_ref) = refs[:count], refs[count:]
    chans, tokens = att_ref.shape
    full = jnp.concatenate([p[...] for p in parts], axis=0)
    turned = reorder(w_ref[...].astype(F32), count).astype(BF16)
    grad = dot(turned, full).astype(BF16)
    z_ref[:chans] = grad
    prod = grad.astype(F32) * att_ref[...]
    for h in range(chans // HEAD_DIM):
        spread = jnp.sum(prod[h * HEAD_DIM : (h + 1) * HEAD_DIM], axis=0, keepdims=True)
        first = chans + h * AUG
        for i in range(tokens // BLOCK):
            t = t_ref[i : i + 1, h * BLOCK : (h + 1) * BLOCK]
            rows = three(ROW_BIAS, ONES) | three(ROW_LSE, split3(-t))
            rows |= three(ROW_SPREAD, split3(-spread[:, lane_block(i)]))
            rows |= {ROW_UP: carry_ref[0, i : i + 1, :], ROW_DOWN: carry_ref[1, i : i + 1, :]}
            z_ref[first : first + AUG, lane_block(i)] = aug_rows(rows, BLOCK)
    rows = z_ref.shape[0]
    both_ref[:rows] = z_ref[...]
    part = reorder(dot_nt(att_ref[...].astype(BF16), full), count)
    high = part.astype(BF16)
    low = (part - high.astype(F32)).astype(BF16)
    for x, places in zip((high, low), part_places(part.shape, tokens, rows)):
        for i, (row, lanes) in enumerate(places):
            both_ref[row : row + AUG, lanes] = x[i * AUG : (i + 1) * AUG]


def part_places(shape, tokens, first):
    per_row = tokens // shape[1]
    tiles = shape[0] // AUG
    terms = []
    for _ in range(2):
        at = [divmod(i, per_row) for i in range(tiles)]
        terms.append(
            [(first + r * AUG, slice(c * shape[1], (c + 1) * shape[1])) for r, c in at]
        )
        first += -(-tiles // per_row) * AUG
    return terms


def parts_kernel(first, mine_ref, came_ref, out_ref):
    shape, tokens = out_ref.shape, mine_ref.shape[1]
    for tile, ends in enumerate(zip(*part_places(shape, tokens, first))):
        total = None
        for ref in (mine_ref, came_ref):
            terms = [ref[row : row + AUG, lanes].astype(F32) for row, lanes in ends]
            total = sum(terms) if total is None else total + sum(terms)
        out_ref[tile * AUG : (tile + 1) * AUG] = total


def query_side(q_ref, z_ref, here):
    chans = q_ref.shape[0]
    heads = chans // HEAD_DIM
    width = heads * BLOCK
    q_wide = spread_heads(q_ref[:, here], heads)
    g_wide = spread_heads(z_ref[:chans, here], heads)
    tiles = [z_ref[chans + h * AUG : chans + (h + 1) * AUG, here] for h in range(heads)]
    aug = jnp.concatenate(tiles, axis=1)
    pad = jnp.zeros((BLOCK - chans - AUG, width), BF16)
    none = jnp.zeros((chans, width), BF16)
    q_aug = jnp.concatenate([q_wide, aug, pad], axis=0)
    g_aug = jnp.concatenate([g_wide, aug, pad], axis=0)
    q_out = jnp.concatenate([q_wide, none], axis=0)
    g_out = jnp.concatenate([none, g_wide], axis=0)
    return q_aug, g_aug, q_out, g_out


def products(side, slots, ka_ref, va_ref):
    q_aug, g_aug = side[:2]
    k_rows = jnp.concatenate([ka_ref[slot] for slot in slots], axis=0)
    v_rows = jnp.concatenate([va_ref[slot] for slot in slots], axis=0)
    probs = jnp.exp2(dot(k_rows, q_aug) * RAW)
    return probs.astype(BF16), (probs * dot(v_rows, g_aug)).astype(BF16)


def pair_grads(side, slots, probs, dlow, acc_ref):
    q_out, g_out = side[2:]
    both = dot_nt(probs, g_out) + dot_nt(dlow, q_out)
    for j, slot in enumerate(slots):
        acc_ref[slot] += both[j * BLOCK : (j + 1) * BLOCK]


def grads_kernel(late, slots_vmem, own_ref, z_ref, ka_ref, va_ref, kn_ref, *refs):
    dq_ref, acc_ref, slots_ref, sems = refs[-4:]
    copies = start_copies((slots_vmem,), (slots_ref,), sems)
    blocks = dq_ref.shape[1] // BLOCK
    heads = dq_ref.shape[0] // HEAD_DIM
    if not late:
        acc_ref[...] = jnp.zeros_like(acc_ref)
    for copy in copies:
        copy.wait()

    def run(count):
        def begin(i):
            slots = [slots_ref[i, j] for j in range(count)]
            side = query_side(own_ref.at[2], z_ref, lane_block(i))
            return side, slots, *products(side, slots, ka_ref, va_ref)

        def finish(i, side, slots, probs, dlow):
            pair_grads(side, slots, probs, dlow, acc_ref)
            dq = dot(jnp.concatenate([kn_ref[slot] for slot in slots], axis=1), dlow)
            dq_ref[:, lane_block(i)] = (pick_heads(dq, heads) * SCALE).astype(BF16)

        cut = EARLY[SIZES.index(count)] * blocks // 8
        in_order(range(cut, blocks) if late else range(cut), begin, finish, 1)

    by_need(slots_ref, run)


def neighbours_kernel(
    dq_in, past_ref, pair_own, other_own, pair_ref, other_ref, ka_ref, va_ref,
    dq_ref, dk_ref, dv_ref, acc_ref, q_all, z_all, lists_vmem, todo_ref, lists_ref, sems,
):
    chans = dk_ref.shape[0]
    blocks = dk_ref.shape[1] // BLOCK
    ext = blocks + 2 * RIM
    odd = lax.rem(lax.axis_index("band"), 2) == 1
    for s, (ref, below) in enumerate(((pair_ref, odd), (other_ref, jnp.logical_not(odd)))):
        rows = ref[chans : chans + AUG].astype(F32)
        row = jnp.where(below, rows[ROW_UP : ROW_UP + 1], rows[ROW_DOWN : ROW_DOWN + 1])
        for i in range(blocks):
            at = s * blocks + i
            lists_vmem[at : at + 1] = row[:, lane_block(i)].astype(jnp.int32)
    lists_vmem[2 * blocks :] = jnp.zeros_like(lists_vmem[2 * blocks :])
    copies = start_copies((lists_vmem,), (lists_ref,), sems)
    q_all[0] = pair_own[2]
    q_all[1] = other_own[2]
    z_all[0] = pair_ref[: z_all.shape[1]]
    z_all[1] = other_ref[...]
    dq_ref[...] = dq_in[...]
    for b in range(blocks):
        acc_ref[RIM + b] = past_ref[RIM + b]
    acc_ref[ext] = past_ref[ext]
    for copy in copies:
        copy.wait()
    step, many = 1, 6
    count = 0
    for row in range(2 * blocks):
        for c in range(0, MAX_KEYS, step):
            todo_ref[count] = row * MAX_KEYS + c
            count = count + (lists_ref[row, c] > 0).astype(jnp.int32)
    for j in range(many):
        todo_ref[count + j] = 2 * blocks * MAX_KEYS

    def body(k, carry):
        begun = []
        for j in range(many):
            todo = todo_ref[k * many + j]
            row, c = todo // MAX_KEYS, todo % MAX_KEYS
            here = pl.ds(pl.multiple_of(row % blocks * BLOCK, BLOCK), BLOCK)
            at = jnp.minimum(row // blocks, 1)
            side = query_side(q_all.at[at], z_all.at[at], here)
            slots = []
            for n in range(step):
                place_of = lists_ref[row, c + n]
                slots.append(jnp.where(place_of > 0, RIM - 1 + place_of, ext))
            begun.append((side, slots, *products(side, slots, ka_ref, va_ref)))
        for one in begun:
            pair_grads(*one, acc_ref)
        return carry

    lax.fori_loop(0, (count + many - 1) // many, body, 0)
    factor = part_factor(2 * chans)
    for b in range(blocks):
        x = (acc_ref[RIM + b] * factor).T
        dk_ref[:, lane_block(b)] = x[:chans].astype(BF16)
        dv_ref[:, lane_block(b)] = x[chans:].astype(BF16)


def part_factor(lanes):
    lane = lax.broadcasted_iota(jnp.int32, (BLOCK, lanes), 1)
    return jnp.where(lane < lanes // 2, SCALE, 1.0).astype(F32)


def kernel_call(body, outs, operands, scalars=(), scratch=(), flops=0, transcendentals=0, aliases=None):
    size = sum(x.size * x.dtype.itemsize for x in operands + outs)
    vmem = pl.BlockSpec(memory_space=pltpu.VMEM)
    copies = [pltpu.SMEM(x.shape, x.dtype) for x in scalars]
    if copies:
        copies.append(pltpu.SemaphoreType.DMA((len(copies),)))
    return pl.pallas_call(
        body,
        out_shape=outs,
        in_specs=[vmem] * len(operands),
        out_specs=[vmem] * len(outs),
        scratch_shapes=list(scratch) + copies,
        input_output_aliases=aliases or {},
        compiler_params=pltpu.CompilerParams(vmem_limit_bytes=VMEM_LIMIT),
        cost_estimate=pl.CostEstimate(
            flops=flops, bytes_accessed=size, transcendentals=transcendentals
        ),
    )(*operands)


def to_pair(value, axis):
    last = lax.axis_size(axis) - 1
    return lax.ppermute(value, axis, [(i, i ^ 1) for i in range(last + 1) if i ^ 1 <= last])


def to_other(value, axis):
    last = lax.axis_size(axis) - 1
    swap = [(i, ((i + 1) ^ 1) - 1) for i in range(last + 1)]
    return lax.ppermute(value, axis, [(i, j) for i, j in swap if 0 <= j <= last])


def gathered(value, axis):
    count = lax.axis_size(axis)
    if count & (count - 1):
        raise ValueError("axis size")
    step, parts = count // 2, {0: value}
    while step:
        swap = [(i, i ^ step) for i in range(count)]
        parts.update({m ^ step: lax.ppermute(x, axis, swap) for m, x in list(parts.items())})
        step //= 2
    return [parts[m] for m in range(count)]


class sum_steps:
    def __init__(self, value, axis):
        self.axis, self.count, self.value, self.came = axis, lax.axis_size(axis), value, None
        self.steps = [1 << i for i in range(self.count.bit_length() - 1)][:0:-1]

    def send(self):
        step = self.steps.pop(0)
        swap = [(i, i ^ step) for i in range(self.count)]
        self.came = lax.ppermute(self.value, self.axis, swap)

    def add(self):
        if self.came is not None:
            shape = jax.ShapeDtypeStruct(self.value.shape, self.value.dtype)
            (self.value,) = kernel_call(add_kernel, [shape], [self.value, self.came])
            self.came = None


def shards(queries, keys, values, grad_out, w_out, key_lists, key_counts):
    chans, tokens = queries.shape
    blocks = tokens // BLOCK
    heads = chans // HEAD_DIM
    ext = blocks + 2 * RIM
    width = heads * BLOCK
    total = tokens * lax.axis_size("band")
    head_count = lax.axis_size("head")
    shape = jax.ShapeDtypeStruct
    pairs = blocks * MAX_KEYS * width * BLOCK

    if blocks != RIM:
        raise ValueError("band size")
    like = lambda x: shape(x.shape, x.dtype)
    own = jnp.stack([keys, values, queries])
    other_own = to_other(own, "band")
    pair_own = to_pair(own, "band")
    parts = gathered(grad_out, "head")
    slots, carry, bias, *state = kernel_call(
        functools.partial(prepare_kernel, total),
        [
            shape((blocks, BLOCK), jnp.int32),
            shape((2, blocks, BLOCK), F32),
            shape((3, ext, BLOCK), F32),
            shape((ext + 1, BLOCK, BLOCK), BF16),
            shape((ext + 1, BLOCK, BLOCK), BF16),
            shape((ext + 1, chans, BLOCK), BF16),
            shape((ext + 1, chans + AUG, BLOCK), BF16),
        ],
        [own, key_lists, key_counts],
        [key_counts],
        scratch=[pltpu.VMEM((blocks, BLOCK), jnp.int32)],
    )
    ka, va, kn, vn, att, t = kernel_call(
        attend_kernel,
        [like(x) for x in state] + [shape((chans, tokens), F32), shape((blocks, width), F32)],
        [slots, own, bias, pair_own, other_own] + state,
        [slots],
        flops=3 * 2 * pairs * BLOCK,
        transcendentals=pairs,
        aliases={5 + i: i for i in range(4)},
    )
    z_rows = chans + heads * AUG
    tail = [AUG + term[-1][0] for term in part_places(w_out.shape, tokens, z_rows)][-1]
    z, z_and_part = kernel_call(
        functools.partial(project_kernel, head_count),
        [shape((z_rows, tokens), BF16), shape((tail, tokens), BF16)],
        [att, t, carry, w_out] + parts,
        flops=4 * w_out.size * tokens,
    )
    pair = to_pair(z_and_part, "band")
    other = to_other(z, "band")
    state = [shape((chans, tokens), BF16), shape((ext + 1, BLOCK, 2 * chans), F32)]
    common = [slots, own, z, ka, va, kn]
    cost = dict(flops=5 * pairs * BLOCK, transcendentals=pairs // 2)
    done = kernel_call(functools.partial(grads_kernel, False), state, common, [slots], **cost)
    done, pair = lax.optimization_barrier((done, pair))
    (part_w,) = kernel_call(
        functools.partial(parts_kernel, z_rows), [shape(w_out.shape, F32)], [z_and_part, pair]
    )
    sums = sum_steps(part_w, "band")
    if sums.steps:
        sums.send()
        done, sums.value = lax.optimization_barrier((done, sums.value))
    done = kernel_call(
        functools.partial(grads_kernel, True),
        state,
        common + list(done),
        [slots],
        aliases={len(common): 0, len(common) + 1: 1},
        **cost,
    )
    if sums.steps:
        done, sums.came = lax.optimization_barrier((done, sums.came))
        sums.add()
        sums.send()
        done, sums.value = lax.optimization_barrier((done, sums.value))
    dq, dk, dv = kernel_call(
        neighbours_kernel,
        [shape((chans, tokens), BF16)] * 3,
        list(done) + [pair_own, other_own, pair, other, ka, va],
        scratch=[
            pltpu.VMEM(state[1].shape, F32),
            pltpu.VMEM((2,) + queries.shape, BF16),
            pltpu.VMEM((2,) + z.shape, BF16),
            pltpu.VMEM((2 * blocks + 8, BLOCK), jnp.int32),
            pltpu.SMEM((2 * blocks * MAX_KEYS + 8,), jnp.int32),
            pltpu.SMEM((2 * blocks + 8, BLOCK), jnp.int32),
            pltpu.SemaphoreType.DMA((1,)),
        ],
        flops=4 * pairs * BLOCK,
        transcendentals=pairs // 2,
    )
    if sums.came is not None:
        dk, sums.came = lax.optimization_barrier((dk, sums.came))
    sums.add()
    while sums.steps:
        sums.send()
        sums.add()
    return (dq, dk, dv, sums.value)


def solution(mesh):
    in_specs = (
        P("head", "band"),
        P("head", "band"),
        P("head", "band"),
        P("head", "band"),
        P("head", None),
        P("band", None),
        P("band"),
    )
    out_specs = (P("head", "band"), P("head", "band"), P("head", "band"), P("head", None))
    return jax.shard_map(shards, mesh=mesh, in_specs=in_specs, out_specs=out_specs, check_vma=False)
```

```python
import functools

import jax
import jax.numpy as jnp
from jax import lax
from jax.experimental import pallas as pl
from jax.experimental.pallas import tpu as pltpu
from jax.sharding import PartitionSpec as P

HEAD_DIM = 32
BLOCK = 128
REACH = 4
MAX_KEYS = 8
RIM = 2 * REACH
SCALE = HEAD_DIM ** (-0.5)
LOG2E = 1.4426950408889634
RAW = SCALE * LOG2E
MASKED = -1e30
AUG = 16
SIZES = (4, 5, 7, MAX_KEYS)
EARLY = (0, 0, 3, 3)
F32 = jnp.float32
BF16 = jnp.bfloat16
VMEM_LIMIT = 48 * 1024 * 1024


def dot(a, b):
    return lax.dot_general(a, b, (((1,), (0,)), ((), ())), preferred_element_type=F32)


def dot_nt(a, b):
    return lax.dot_general(a, b, (((1,), (1,)), ((), ())), preferred_element_type=F32)


def split3(x):
    hi = x.astype(BF16).astype(F32)
    rest = x - hi
    mid = rest.astype(BF16).astype(F32)
    return hi, mid, (rest - mid).astype(BF16).astype(F32)


def aug_rows(rows, width):
    at = lax.broadcasted_iota(jnp.int32, (AUG, width), 0)
    out = jnp.zeros((AUG, width), F32)
    for i, row in rows.items():
        out = jnp.where(at == i, row, out)
    return out.astype(BF16)


ROW_LSE, ROW_SPREAD, ROW_BIAS = 0, 3, 6
PER_HEAD = 6


def three(first, rows):
    return {first + i: row for i, row in enumerate(rows)}


ONES = (1.0, 1.0, 1.0)


def spread_heads(x, heads):
    zero = jnp.zeros((HEAD_DIM, BLOCK), x.dtype)
    rows = []
    for h in range(heads):
        part = x[h * HEAD_DIM : (h + 1) * HEAD_DIM]
        rows.append(jnp.concatenate([part if g == h else zero for g in range(heads)], axis=1))
    return jnp.concatenate(rows, axis=0)


def pick_heads(x, heads):
    return jnp.concatenate(
        [
            x[h * HEAD_DIM : (h + 1) * HEAD_DIM, h * BLOCK : (h + 1) * BLOCK]
            for h in range(heads)
        ],
        axis=0,
    )


def lane_block(i):
    return slice(i * BLOCK, (i + 1) * BLOCK)


def start_copies(srcs, dsts, sems):
    copies = [pltpu.make_async_copy(s, d, sems.at[i]) for i, (s, d) in enumerate(zip(srcs, dsts))]
    for copy in copies:
        copy.start()
    return copies


def rim_bases(blocks):
    odd = lax.rem(lax.axis_index("band"), 2) == 1
    low, high = 0, RIM + blocks
    return jnp.where(odd, low, high), jnp.where(odd, high, low)


def rim_bases(blocks):
    odd = lax.rem(lax.axis_index("band"), 2) == 1
    low, high = 0, RIM + blocks
    return jnp.where(odd, low, high), jnp.where(odd, high, low)


def in_order(steps, begin, finish, ahead):
    begun = []
    for n, step in enumerate(steps):
        while len(begun) <= ahead and n + len(begun) < len(steps):
            begun.append(begin(steps[n + len(begun)]))
        finish(step, *begun.pop(0))


def place(refs, b, k_blk, v_blk, bias):
    ka_ref, va_ref, kn_ref, vn_ref = refs
    pad = jnp.zeros((BLOCK - k_blk.shape[0] - AUG, BLOCK), BF16)
    k_aug = aug_rows(three(ROW_BIAS, bias) | three(ROW_LSE, ONES), BLOCK)
    v_with = jnp.concatenate([v_blk, aug_rows(three(ROW_SPREAD, ONES), BLOCK)], axis=0)
    kn_ref[b] = k_blk
    vn_ref[b] = v_with
    ka_ref[b] = jnp.concatenate([k_blk, k_aug, pad], axis=0).T
    va_ref[b] = jnp.concatenate([v_with, pad], axis=0).T


def by_need(slots_ref, run):
    most = slots_ref[0, MAX_KEYS]
    for low, high in zip((0,) + SIZES, SIZES):
        pl.when(jnp.logical_and(most > low, most <= high))(functools.partial(run, high))


def add_kernel(a_ref, b_ref, out_ref):
    out_ref[...] = (a_ref[...].astype(F32) + b_ref[...].astype(F32)).astype(out_ref.dtype)


def packed(chosen, values):
    shape = values.shape
    lane = lax.broadcasted_iota(jnp.int32, shape, 1)
    before = (
        lax.broadcasted_iota(jnp.int32, (BLOCK, BLOCK), 0)
        < lax.broadcasted_iota(jnp.int32, (BLOCK, BLOCK), 1)
    )
    rank = dot(chosen.astype(F32), before.astype(F32))
    out = jnp.zeros(shape, F32)
    for r in range(MAX_KEYS):
        hit = jnp.logical_and(chosen, rank == r)
        value = jnp.sum(jnp.where(hit, values.astype(F32) + 1.0, 0.0), axis=1, keepdims=True)
        out = jnp.where(lane == r, value, out)
    return out


def prepare_kernel(
    total, own_ref, lists_ref, counts_ref,
    slots_ref, carry_ref, bias_ref, acc_ref, ka_ref, va_ref, kn_ref, vn_ref,
    wide_ref, counts_smem, sems,
):
    copies = start_copies((counts_ref,), (counts_smem,), sems)
    acc_ref[...] = jnp.zeros_like(acc_ref)
    chans = own_ref.shape[1]
    blocks = own_ref.shape[2] // BLOCK
    ext = blocks + 2 * RIM
    first_block = lax.axis_index("band") * blocks - RIM
    at = lax.broadcasted_iota(jnp.int32, (ext, BLOCK), 0) * BLOCK
    at = at + lax.broadcasted_iota(jnp.int32, (ext, BLOCK), 1) + first_block * BLOCK
    at = jnp.clip(at, 0, total - 1).astype(F32)
    logw = jnp.log(jnp.sin(jnp.pi * (at + 0.5) / total))
    bias = split3(logw * (1.0 / SCALE))
    for i, part in enumerate(bias):
        bias_ref[i] = part
    refs = (ka_ref, va_ref, kn_ref, vn_ref)
    none = jnp.zeros((chans, BLOCK), BF16)
    place(refs, ext, none, none, [MASKED, 0.0, 0.0])
    for b in range(blocks):
        rows = [part[RIM + b : RIM + b + 1] for part in bias]
        place(refs, RIM + b, own_ref[0, :, lane_block(b)], own_ref[1, :, lane_block(b)], rows)
    for copy in copies:
        copy.wait()
    wide_ref[...] = jnp.zeros_like(wide_ref)
    wide_ref[:, :MAX_KEYS] = lists_ref[...]
    lane = lax.broadcasted_iota(jnp.int32, (blocks, BLOCK), 1)
    row = lax.broadcasted_iota(jnp.int32, (blocks, BLOCK), 0)
    used, most = jnp.zeros((blocks, BLOCK), jnp.int32), 0
    for i in range(blocks):
        used = jnp.where(row == i, counts_smem[i], used)
        most = jnp.maximum(most, counts_smem[i])
    slots = jnp.where(lane < used, wide_ref[...] - first_block, ext)
    slots_ref[...] = jnp.where(lane == MAX_KEYS, most, slots)
    upper = RIM + blocks
    carry_ref[0] = packed(jnp.logical_and(slots >= upper, slots < ext), slots - upper)
    carry_ref[1] = packed(slots < RIM, slots)


def attend_kernel(
    slots_vmem, own_ref, bias_ref, pair_ref, other_ref, ka_in, va_in, kn_in, vn_in,
    ka_ref, va_ref, kn_ref, vn_ref, att_ref, t_ref, slots_ref, sems,
):
    copies = start_copies((slots_vmem,), (slots_ref,), sems)
    chans = own_ref.shape[1]
    heads = chans // HEAD_DIM
    blocks = own_ref.shape[2] // BLOCK
    width = heads * BLOCK
    refs = (ka_ref, va_ref, kn_ref, vn_ref)
    for base, ref in zip(rim_bases(blocks), (pair_ref, other_ref)):
        for b in range(RIM):
            rows = [bias_ref[i, pl.ds(base + b, 1), :] for i in range(3)]
            place(refs, base + b, ref[0, :, lane_block(b)], ref[1, :, lane_block(b)], rows)
    for copy in copies:
        copy.wait()

    ones = aug_rows(three(ROW_BIAS, ONES), width)
    pad_w = jnp.zeros((BLOCK - chans - AUG, width), BF16)

    def scores(i):
        q_aug = jnp.concatenate([spread_heads(own_ref[2, :, lane_block(i)], heads), ones, pad_w], axis=0)
        slots = [slots_ref[i, j] for j in range(MAX_KEYS)]
        k_rows = jnp.concatenate([ka_ref[slot] for slot in slots], axis=0)
        s = dot(k_rows, q_aug)
        peak = jnp.max(jnp.max(s.reshape(-1, 8, width), axis=0), axis=0, keepdims=True)
        return slots, s, peak

    def finish(i, slots, s, peak):
        e = jnp.exp2((s - peak) * RAW)
        v_cols = jnp.concatenate([vn_ref[slot] for slot in slots], axis=1)
        acc = dot(v_cols, e.astype(BF16))
        whole = acc[chans + ROW_SPREAD : chans + ROW_SPREAD + 1]
        att_ref[:, lane_block(i)] = pick_heads(acc[:chans] * (1.0 / whole), heads)
        t_ref[i : i + 1] = peak + jnp.log2(whole) * (1.0 / RAW)

    in_order(range(blocks), scores, finish, 2)


def reorder(x, count):
    depth = x.shape[1] // count
    here = lax.axis_index("head")
    bit = 1
    while bit < count:
        parts = [x[:, (m ^ bit) * depth : ((m ^ bit) + 1) * depth] for m in range(count)]
        x = jnp.where((here & bit) != 0, jnp.concatenate(parts, axis=1), x)
        bit *= 2
    return x


def project_kernel(
    count, slots_vmem, own_ref, att_ref, t_ref, carry_ref, w_ref, ka_ref, va_ref, kn_ref, acc_in, *refs
):
    parts, (z_ref, both_ref, dq_ref, acc_ref, slots_ref, sems) = refs[:count], refs[count:]
    copies = start_copies((slots_vmem,), (slots_ref,), sems)
    chans, tokens = att_ref.shape
    full = jnp.concatenate([p[...] for p in parts], axis=0)
    turned = reorder(w_ref[...].astype(F32), count).astype(BF16)
    grad = dot(turned, full).astype(BF16)
    z_ref[:chans] = grad
    prod = grad.astype(F32) * att_ref[...]
    heads = chans // HEAD_DIM
    spreads = [
        jnp.sum(prod[h * HEAD_DIM : (h + 1) * HEAD_DIM], axis=0, keepdims=True)
        for h in range(heads)
    ]
    for i in range(tokens // BLOCK):
        rows = {}
        for h in range(heads):
            t = t_ref[i : i + 1, h * BLOCK : (h + 1) * BLOCK]
            rows |= three(PER_HEAD * h + ROW_LSE, split3(-t))
            rows |= three(PER_HEAD * h + ROW_SPREAD, split3(-spreads[h][:, lane_block(i)]))
        rows |= {PER_HEAD * heads + s: carry_ref[s, i : i + 1, :] for s in range(2)}
        z_ref[chans:, lane_block(i)] = aug_rows(rows, BLOCK)
    rows = z_ref.shape[0]
    both_ref[:rows] = z_ref[...]
    part = reorder(dot_nt(att_ref[...].astype(BF16), full), count)
    high = part.astype(BF16)
    low = (part - high.astype(F32)).astype(BF16)
    for x, places in zip((high, low), part_places(part.shape, tokens, rows)):
        for i, (row, lanes) in enumerate(places):
            both_ref[row : row + AUG, lanes] = x[i * AUG : (i + 1) * AUG]
    for copy in copies:
        copy.wait()
    blocks = tokens // BLOCK

    def run(most):
        steps = range(EARLY[SIZES.index(most)] * blocks // 8)
        if steps:
            block_grads(
                steps, most, own_ref, z_ref, ka_ref, va_ref, kn_ref, dq_ref, acc_ref, slots_ref
            )

    by_need(slots_ref, run)


def part_places(shape, tokens, first):
    per_row = tokens // shape[1]
    tiles = shape[0] // AUG
    terms = []
    for _ in range(2):
        at = [divmod(i, per_row) for i in range(tiles)]
        terms.append(
            [(first + r * AUG, slice(c * shape[1], (c + 1) * shape[1])) for r, c in at]
        )
        first += -(-tiles // per_row) * AUG
    return terms


def parts_kernel(first, mine_ref, came_ref, out_ref):
    shape, tokens = out_ref.shape, mine_ref.shape[1]
    for tile, ends in enumerate(zip(*part_places(shape, tokens, first))):
        total = None
        for ref in (mine_ref, came_ref):
            terms = [ref[row : row + AUG, lanes].astype(F32) for row, lanes in ends]
            total = sum(terms) if total is None else total + sum(terms)
        out_ref[tile * AUG : (tile + 1) * AUG] = total


def query_side(q_ref, z_ref, here):
    chans = q_ref.shape[0]
    heads = chans // HEAD_DIM
    width = heads * BLOCK
    q_wide = spread_heads(q_ref[:, here], heads)
    g_wide = spread_heads(z_ref[:chans, here], heads)
    tile = z_ref[chans:, here].astype(F32)
    at = lax.broadcasted_iota(jnp.int32, tile.shape, 0)
    ones = jnp.logical_and(at >= ROW_BIAS, at < ROW_BIAS + 3)
    tiles = [tile] + [pltpu.roll(tile, AUG - PER_HEAD * h, 0) for h in range(1, heads)]
    aug = jnp.concatenate([jnp.where(ones, 1.0, x).astype(BF16) for x in tiles], axis=1)
    pad = jnp.zeros((BLOCK - chans - AUG, width), BF16)
    none = jnp.zeros((chans, width), BF16)
    q_aug = jnp.concatenate([q_wide, aug, pad], axis=0)
    g_aug = jnp.concatenate([g_wide, aug, pad], axis=0)
    q_out = jnp.concatenate([q_wide, none], axis=0)
    g_out = jnp.concatenate([none, g_wide], axis=0)
    return q_aug, g_aug, q_out, g_out


def products(side, slots, ka_ref, va_ref):
    q_aug, g_aug = side[:2]
    k_rows = jnp.concatenate([ka_ref[slot] for slot in slots], axis=0)
    v_rows = jnp.concatenate([va_ref[slot] for slot in slots], axis=0)
    probs = jnp.exp2(dot(k_rows, q_aug) * RAW)
    return probs.astype(BF16), (probs * dot(v_rows, g_aug)).astype(BF16)


def pair_grads(side, slots, probs, dlow, acc_ref):
    q_out, g_out = side[2:]
    both = dot_nt(probs, g_out) + dot_nt(dlow, q_out)
    for j, slot in enumerate(slots):
        acc_ref[slot] += both[j * BLOCK : (j + 1) * BLOCK]


def block_grads(steps, count, own_ref, z_ref, ka_ref, va_ref, kn_ref, dq_ref, acc_ref, slots_ref):
    heads = dq_ref.shape[0] // HEAD_DIM

    def begin(i):
        slots = [slots_ref[i, j] for j in range(count)]
        side = query_side(own_ref.at[2], z_ref, lane_block(i))
        return side, slots, *products(side, slots, ka_ref, va_ref)

    def finish(i, side, slots, probs, dlow):
        pair_grads(side, slots, probs, dlow, acc_ref)
        dq = dot(jnp.concatenate([kn_ref[slot] for slot in slots], axis=1), dlow)
        dq_ref[:, lane_block(i)] = (pick_heads(dq, heads) * SCALE).astype(BF16)

    in_order(steps, begin, finish, 1)


def grads_kernel(
    slots_vmem, own_ref, z_ref, ka_ref, va_ref, kn_ref, dq_in, acc_in,
    dq_ref, acc_ref, slots_ref, sems,
):
    copies = start_copies((slots_vmem,), (slots_ref,), sems)
    blocks = dq_ref.shape[1] // BLOCK
    for copy in copies:
        copy.wait()

    def run(most):
        steps = range(EARLY[SIZES.index(most)] * blocks // 8, blocks)
        block_grads(
            steps, most, own_ref, z_ref, ka_ref, va_ref, kn_ref, dq_ref, acc_ref, slots_ref
        )

    by_need(slots_ref, run)


def neighbours_kernel(
    dq_in, past_ref, pair_own, other_own, pair_ref, other_ref, ka_ref, va_ref,
    dq_ref, dk_ref, dv_ref, acc_ref, q_all, z_all, lists_vmem, todo_ref, lists_ref, sems,
):
    chans = dk_ref.shape[0]
    blocks = dk_ref.shape[1] // BLOCK
    ext = blocks + 2 * RIM
    odd = lax.rem(lax.axis_index("band"), 2) == 1
    for s, (ref, below) in enumerate(((pair_ref, odd), (other_ref, jnp.logical_not(odd)))):
        rows = ref[chans : chans + AUG].astype(F32)
        up = PER_HEAD * (chans // HEAD_DIM)
        row = jnp.where(below, rows[up : up + 1], rows[up + 1 : up + 2])
        for i in range(blocks):
            at = s * blocks + i
            lists_vmem[at : at + 1] = row[:, lane_block(i)].astype(jnp.int32)
    lists_vmem[2 * blocks :] = jnp.zeros_like(lists_vmem[2 * blocks :])
    copies = start_copies((lists_vmem,), (lists_ref,), sems)
    q_all[0] = pair_own[2]
    q_all[1] = other_own[2]
    z_all[0] = pair_ref[: z_all.shape[1]]
    z_all[1] = other_ref[...]
    dq_ref[...] = dq_in[...]
    for b in range(blocks):
        acc_ref[RIM + b] = past_ref[RIM + b]
    acc_ref[ext] = past_ref[ext]
    for copy in copies:
        copy.wait()
    step, many = 1, 6
    count = 0
    for row in range(2 * blocks):
        for c in range(0, MAX_KEYS, step):
            todo_ref[count] = row * MAX_KEYS + c
            count = count + (lists_ref[row, c] > 0).astype(jnp.int32)
    for j in range(many):
        todo_ref[count + j] = 2 * blocks * MAX_KEYS

    def body(k, carry):
        begun = []
        for j in range(many):
            todo = todo_ref[k * many + j]
            row, c = todo // MAX_KEYS, todo % MAX_KEYS
            here = pl.ds(pl.multiple_of(row % blocks * BLOCK, BLOCK), BLOCK)
            at = jnp.minimum(row // blocks, 1)
            side = query_side(q_all.at[at], z_all.at[at], here)
            slots = []
            for n in range(step):
                place_of = lists_ref[row, c + n]
                slots.append(jnp.where(place_of > 0, RIM - 1 + place_of, ext))
            begun.append((side, slots, *products(side, slots, ka_ref, va_ref)))
        for one in begun:
            pair_grads(*one, acc_ref)
        return carry

    lax.fori_loop(0, (count + many - 1) // many, body, 0)
    factor = part_factor(2 * chans)
    for b in range(blocks):
        x = (acc_ref[RIM + b] * factor).T
        dk_ref[:, lane_block(b)] = x[:chans].astype(BF16)
        dv_ref[:, lane_block(b)] = x[chans:].astype(BF16)


def part_factor(lanes):
    lane = lax.broadcasted_iota(jnp.int32, (BLOCK, lanes), 1)
    return jnp.where(lane < lanes // 2, SCALE, 1.0).astype(F32)


def kernel_call(body, outs, operands, scalars=(), scratch=(), flops=0, transcendentals=0, aliases=None):
    size = sum(x.size * x.dtype.itemsize for x in operands + outs)
    vmem = pl.BlockSpec(memory_space=pltpu.VMEM)
    copies = [pltpu.SMEM(x.shape, x.dtype) for x in scalars]
    if copies:
        copies.append(pltpu.SemaphoreType.DMA((len(copies),)))
    return pl.pallas_call(
        body,
        out_shape=outs,
        in_specs=[vmem] * len(operands),
        out_specs=[vmem] * len(outs),
        scratch_shapes=list(scratch) + copies,
        input_output_aliases=aliases or {},
        compiler_params=pltpu.CompilerParams(vmem_limit_bytes=VMEM_LIMIT),
        cost_estimate=pl.CostEstimate(
            flops=flops, bytes_accessed=size, transcendentals=transcendentals
        ),
    )(*operands)


def to_pair(value, axis):
    last = lax.axis_size(axis) - 1
    return lax.ppermute(value, axis, [(i, i ^ 1) for i in range(last + 1) if i ^ 1 <= last])


def to_other(value, axis):
    last = lax.axis_size(axis) - 1
    swap = [(i, ((i + 1) ^ 1) - 1) for i in range(last + 1)]
    return lax.ppermute(value, axis, [(i, j) for i, j in swap if 0 <= j <= last])


def gathered(value, axis):
    count = lax.axis_size(axis)
    if count & (count - 1):
        raise ValueError("axis size")
    step, parts = count // 2, {0: value}
    while step:
        swap = [(i, i ^ step) for i in range(count)]
        parts.update({m ^ step: lax.ppermute(x, axis, swap) for m, x in list(parts.items())})
        step //= 2
    return [parts[m] for m in range(count)]


class sum_steps:
    def __init__(self, value, axis):
        self.axis, self.count, self.value, self.came = axis, lax.axis_size(axis), value, None
        self.steps = [1 << i for i in range(self.count.bit_length() - 1)][:0:-1]

    def send(self):
        step = self.steps.pop(0)
        swap = [(i, i ^ step) for i in range(self.count)]
        self.came = lax.ppermute(self.value, self.axis, swap)

    def add(self):
        if self.came is not None:
            kind = BF16 if len(self.steps) == 1 else F32
            shape = jax.ShapeDtypeStruct(self.value.shape, kind)
            (self.value,) = kernel_call(add_kernel, [shape], [self.value, self.came])
            self.came = None


def shards(queries, keys, values, grad_out, w_out, key_lists, key_counts):
    chans, tokens = queries.shape
    blocks = tokens // BLOCK
    heads = chans // HEAD_DIM
    ext = blocks + 2 * RIM
    width = heads * BLOCK
    total = tokens * lax.axis_size("band")
    head_count = lax.axis_size("head")
    shape = jax.ShapeDtypeStruct
    pairs = blocks * MAX_KEYS * width * BLOCK

    if blocks != RIM or PER_HEAD * heads + 2 > AUG:
        raise ValueError("band size")
    like = lambda x: shape(x.shape, x.dtype)
    own = jnp.stack([keys, values, queries])
    other_own = to_other(own, "band")
    pair_own = to_pair(own, "band")
    parts = gathered(grad_out, "head")
    slots, carry, bias, acc, *state = kernel_call(
        functools.partial(prepare_kernel, total),
        [
            shape((blocks, BLOCK), jnp.int32),
            shape((2, blocks, BLOCK), F32),
            shape((3, ext, BLOCK), F32),
            shape((ext + 1, BLOCK, 2 * chans), F32),
            shape((ext + 1, BLOCK, BLOCK), BF16),
            shape((ext + 1, BLOCK, BLOCK), BF16),
            shape((ext + 1, chans, BLOCK), BF16),
            shape((ext + 1, chans + AUG, BLOCK), BF16),
        ],
        [own, key_lists, key_counts],
        [key_counts],
        scratch=[pltpu.VMEM((blocks, BLOCK), jnp.int32)],
    )
    ka, va, kn, vn, att, t = kernel_call(
        attend_kernel,
        [like(x) for x in state] + [shape((chans, tokens), F32), shape((blocks, width), F32)],
        [slots, own, bias, pair_own, other_own] + state,
        [slots],
        flops=3 * 2 * pairs * BLOCK,
        transcendentals=pairs,
        aliases={5 + i: i for i in range(4)},
    )
    z_rows = chans + AUG
    tail = [AUG + term[-1][0] for term in part_places(w_out.shape, tokens, z_rows)][-1]
    data = [ka, va, kn]
    operands = [slots, own, att, t, carry, w_out] + data + [acc]
    z, z_and_part, *done = kernel_call(
        functools.partial(project_kernel, head_count),
        [shape((z_rows, tokens), BF16), shape((tail, tokens), BF16), like(queries), like(acc)],
        operands + parts,
        [slots],
        flops=4 * w_out.size * tokens,
        aliases={len(operands) - 1: 3},
    )
    pair = to_pair(z_and_part, "band")
    other = to_other(z, "band")
    done, pair = lax.optimization_barrier((done, pair))
    (part_w,) = kernel_call(
        functools.partial(parts_kernel, z_rows), [shape(w_out.shape, F32)], [z_and_part, pair]
    )
    sums = sum_steps(part_w, "band")
    if sums.steps:
        sums.send()
        done, sums.value = lax.optimization_barrier((done, sums.value))
    done = kernel_call(
        grads_kernel,
        [like(x) for x in done],
        [slots, own, z] + data + list(done),
        [slots],
        flops=10 * pairs * BLOCK,
        transcendentals=pairs,
        aliases={6: 0, 7: 1},
    )
    if sums.steps:
        done, sums.came = lax.optimization_barrier((done, sums.came))
        sums.add()
        sums.send()
        done, sums.value = lax.optimization_barrier((done, sums.value))
    dq, dk, dv = kernel_call(
        neighbours_kernel,
        [shape((chans, tokens), BF16)] * 3,
        list(done) + [pair_own, other_own, pair, other, ka, va],
        scratch=[
            pltpu.VMEM(acc.shape, F32),
            pltpu.VMEM((2,) + queries.shape, BF16),
            pltpu.VMEM((2,) + z.shape, BF16),
            pltpu.VMEM((2 * blocks + 8, BLOCK), jnp.int32),
            pltpu.SMEM((2 * blocks * MAX_KEYS + 8,), jnp.int32),
            pltpu.SMEM((2 * blocks + 8, BLOCK), jnp.int32),
            pltpu.SemaphoreType.DMA((1,)),
        ],
        flops=4 * pairs * BLOCK,
        transcendentals=pairs // 2,
    )
    if sums.came is not None:
        dk, sums.came = lax.optimization_barrier((dk, sums.came))
    sums.add()
    while sums.steps:
        sums.send()
        sums.add()
    return (dq, dk, dv, sums.value)


def solution(mesh):
    in_specs = (
        P("head", "band"),
        P("head", "band"),
        P("head", "band"),
        P("head", "band"),
        P("head", None),
        P("band", None),
        P("band"),
    )
    out_specs = (P("head", "band"), P("head", "band"), P("head", "band"), P("head", None))
    return jax.shard_map(shards, mesh=mesh, in_specs=in_specs, out_specs=out_specs, check_vma=False)
```

```python
import functools

import jax
import jax.numpy as jnp
from jax import lax
from jax.experimental import pallas as pl
from jax.experimental.pallas import tpu as pltpu
from jax.sharding import PartitionSpec as P

HEAD_DIM = 32
BLOCK = 128
REACH = 4
MAX_KEYS = 8
RIM = 2 * REACH
SCALE = HEAD_DIM ** (-0.5)
LOG2E = 1.4426950408889634
RAW = SCALE * LOG2E
MASKED = -1e30
AUG = 16
SIZES = (4, 5, 7, MAX_KEYS)
EARLY = (0, 0, 3, 4)
F32 = jnp.float32
BF16 = jnp.bfloat16
VMEM_LIMIT = 48 * 1024 * 1024


def dot(a, b):
    return lax.dot_general(a, b, (((1,), (0,)), ((), ())), preferred_element_type=F32)


def dot_nt(a, b):
    return lax.dot_general(a, b, (((1,), (1,)), ((), ())), preferred_element_type=F32)


def split3(x):
    hi = x.astype(BF16).astype(F32)
    rest = x - hi
    mid = rest.astype(BF16).astype(F32)
    return hi, mid, (rest - mid).astype(BF16).astype(F32)


def aug_rows(rows, width):
    at = lax.broadcasted_iota(jnp.int32, (AUG, width), 0)
    out = jnp.zeros((AUG, width), F32)
    for i, row in rows.items():
        out = jnp.where(at == i, row, out)
    return out.astype(BF16)


ROW_LSE, ROW_SPREAD, ROW_BIAS = 0, 3, 6
PER_HEAD = 6


def three(first, rows):
    return {first + i: row for i, row in enumerate(rows)}


ONES = (1.0, 1.0, 1.0)


def spread_heads(x, heads):
    zero = jnp.zeros((HEAD_DIM, BLOCK), x.dtype)
    rows = []
    for h in range(heads):
        part = x[h * HEAD_DIM : (h + 1) * HEAD_DIM]
        rows.append(jnp.concatenate([part if g == h else zero for g in range(heads)], axis=1))
    return jnp.concatenate(rows, axis=0)


def pick_heads(x, heads):
    return jnp.concatenate(
        [
            x[h * HEAD_DIM : (h + 1) * HEAD_DIM, h * BLOCK : (h + 1) * BLOCK]
            for h in range(heads)
        ],
        axis=0,
    )


def lane_block(i):
    return slice(i * BLOCK, (i + 1) * BLOCK)


def start_copies(srcs, dsts, sems):
    copies = [pltpu.make_async_copy(s, d, sems.at[i]) for i, (s, d) in enumerate(zip(srcs, dsts))]
    for copy in copies:
        copy.start()
    return copies


def rim_bases(blocks):
    odd = lax.rem(lax.axis_index("band"), 2) == 1
    low, high = 0, RIM + blocks
    return jnp.where(odd, low, high), jnp.where(odd, high, low)


def rim_bases(blocks):
    odd = lax.rem(lax.axis_index("band"), 2) == 1
    low, high = 0, RIM + blocks
    return jnp.where(odd, low, high), jnp.where(odd, high, low)


def in_order(steps, begin, finish, ahead):
    begun = []
    for n, step in enumerate(steps):
        while len(begun) <= ahead and n + len(begun) < len(steps):
            begun.append(begin(steps[n + len(begun)]))
        finish(step, *begun.pop(0))


def place(refs, b, k_blk, v_blk, bias):
    ka_ref, va_ref, kn_ref, vn_ref = refs
    pad = jnp.zeros((BLOCK - k_blk.shape[0] - AUG, BLOCK), BF16)
    k_aug = aug_rows(three(ROW_BIAS, bias) | three(ROW_LSE, ONES), BLOCK)
    v_with = jnp.concatenate([v_blk, aug_rows(three(ROW_SPREAD, ONES), BLOCK)], axis=0)
    kn_ref[b] = k_blk
    vn_ref[b] = v_with
    ka_ref[b] = jnp.concatenate([k_blk, k_aug, pad], axis=0).T
    va_ref[b] = jnp.concatenate([v_with, pad], axis=0).T


def by_need(slots_ref, run):
    most = slots_ref[0, MAX_KEYS]
    for low, high in zip((0,) + SIZES, SIZES):
        pl.when(jnp.logical_and(most > low, most <= high))(functools.partial(run, high))


def add_kernel(a_ref, b_ref, out_ref):
    out_ref[...] = (a_ref[...].astype(F32) + b_ref[...].astype(F32)).astype(out_ref.dtype)


def packed(chosen, values):
    shape = values.shape
    lane = lax.broadcasted_iota(jnp.int32, shape, 1)
    before = (
        lax.broadcasted_iota(jnp.int32, (BLOCK, BLOCK), 0)
        < lax.broadcasted_iota(jnp.int32, (BLOCK, BLOCK), 1)
    )
    rank = dot(chosen.astype(F32), before.astype(F32))
    out = jnp.zeros(shape, F32)
    for r in range(MAX_KEYS):
        hit = jnp.logical_and(chosen, rank == r)
        value = jnp.sum(jnp.where(hit, values.astype(F32) + 1.0, 0.0), axis=1, keepdims=True)
        out = jnp.where(lane == r, value, out)
    return out


def prepare_kernel(
    total, own_ref, lists_ref, counts_ref,
    slots_ref, carry_ref, bias_ref, acc_ref, ka_ref, va_ref, kn_ref, vn_ref,
    wide_ref, counts_smem, sems,
):
    copies = start_copies((counts_ref,), (counts_smem,), sems)
    acc_ref[...] = jnp.zeros_like(acc_ref)
    chans = own_ref.shape[1]
    blocks = own_ref.shape[2] // BLOCK
    ext = blocks + 2 * RIM
    first_block = lax.axis_index("band") * blocks - RIM
    at = lax.broadcasted_iota(jnp.int32, (ext, BLOCK), 0) * BLOCK
    at = at + lax.broadcasted_iota(jnp.int32, (ext, BLOCK), 1) + first_block * BLOCK
    at = jnp.clip(at, 0, total - 1).astype(F32)
    logw = jnp.log(jnp.sin(jnp.pi * (at + 0.5) / total))
    bias = split3(logw * (1.0 / SCALE))
    for i, part in enumerate(bias):
        bias_ref[i] = part
    refs = (ka_ref, va_ref, kn_ref, vn_ref)
    none = jnp.zeros((chans, BLOCK), BF16)
    place(refs, ext, none, none, [MASKED, 0.0, 0.0])
    for b in range(blocks):
        rows = [part[RIM + b : RIM + b + 1] for part in bias]
        place(refs, RIM + b, own_ref[0, :, lane_block(b)], own_ref[1, :, lane_block(b)], rows)
    for copy in copies:
        copy.wait()
    wide_ref[...] = jnp.zeros_like(wide_ref)
    wide_ref[:, :MAX_KEYS] = lists_ref[...]
    lane = lax.broadcasted_iota(jnp.int32, (blocks, BLOCK), 1)
    row = lax.broadcasted_iota(jnp.int32, (blocks, BLOCK), 0)
    used, most = jnp.zeros((blocks, BLOCK), jnp.int32), 0
    for i in range(blocks):
        used = jnp.where(row == i, counts_smem[i], used)
        most = jnp.maximum(most, counts_smem[i])
    slots = jnp.where(lane < used, wide_ref[...] - first_block, ext)
    slots_ref[...] = jnp.where(lane == MAX_KEYS, most, slots)
    upper = RIM + blocks
    carry_ref[0] = packed(jnp.logical_and(slots >= upper, slots < ext), slots - upper)
    carry_ref[1] = packed(slots < RIM, slots)


def attend_kernel(
    slots_vmem, own_ref, bias_ref, pair_ref, other_ref, ka_in, va_in, kn_in, vn_in,
    ka_ref, va_ref, kn_ref, vn_ref, att_ref, t_ref, slots_ref, sems,
):
    copies = start_copies((slots_vmem,), (slots_ref,), sems)
    chans = own_ref.shape[1]
    heads = chans // HEAD_DIM
    blocks = own_ref.shape[2] // BLOCK
    width = heads * BLOCK
    refs = (ka_ref, va_ref, kn_ref, vn_ref)
    for base, ref in zip(rim_bases(blocks), (pair_ref, other_ref)):
        for b in range(RIM):
            rows = [bias_ref[i, pl.ds(base + b, 1), :] for i in range(3)]
            place(refs, base + b, ref[0, :, lane_block(b)], ref[1, :, lane_block(b)], rows)
    for copy in copies:
        copy.wait()

    ones = aug_rows(three(ROW_BIAS, ONES), width)
    pad_w = jnp.zeros((BLOCK - chans - AUG, width), BF16)

    def scores(i):
        q_aug = jnp.concatenate([spread_heads(own_ref[2, :, lane_block(i)], heads), ones, pad_w], axis=0)
        slots = [slots_ref[i, j] for j in range(MAX_KEYS)]
        k_rows = jnp.concatenate([ka_ref[slot] for slot in slots], axis=0)
        s = dot(k_rows, q_aug)
        peak = jnp.max(jnp.max(s.reshape(-1, 8, width), axis=0), axis=0, keepdims=True)
        return slots, s, peak

    def finish(i, slots, s, peak):
        e = jnp.exp2((s - peak) * RAW)
        v_cols = jnp.concatenate([vn_ref[slot] for slot in slots], axis=1)
        acc = dot(v_cols, e.astype(BF16))
        whole = acc[chans + ROW_SPREAD : chans + ROW_SPREAD + 1]
        att_ref[:, lane_block(i)] = pick_heads(acc[:chans] * (1.0 / whole), heads)
        t_ref[i : i + 1] = peak + jnp.log2(whole) * (1.0 / RAW)

    in_order(range(blocks), scores, finish, 2)


def reorder(x, count):
    depth = x.shape[1] // count
    here = lax.axis_index("head")
    bit = 1
    while bit < count:
        parts = [x[:, (m ^ bit) * depth : ((m ^ bit) + 1) * depth] for m in range(count)]
        x = jnp.where((here & bit) != 0, jnp.concatenate(parts, axis=1), x)
        bit *= 2
    return x


def project_kernel(
    count, slots_vmem, own_ref, att_ref, t_ref, carry_ref, w_ref, ka_ref, va_ref, kn_ref, acc_in, *refs
):
    parts, (z_ref, both_ref, dq_ref, acc_ref, slots_ref, sems) = refs[:count], refs[count:]
    copies = start_copies((slots_vmem,), (slots_ref,), sems)
    chans, tokens = att_ref.shape
    full = jnp.concatenate([p[...] for p in parts], axis=0)
    turned = reorder(w_ref[...].astype(F32), count).astype(BF16)
    grad = dot(turned, full).astype(BF16)
    z_ref[:chans] = grad
    prod = grad.astype(F32) * att_ref[...]
    heads = chans // HEAD_DIM
    spreads = [
        jnp.sum(prod[h * HEAD_DIM : (h + 1) * HEAD_DIM], axis=0, keepdims=True)
        for h in range(heads)
    ]
    for i in range(tokens // BLOCK):
        rows = {}
        for h in range(heads):
            t = t_ref[i : i + 1, h * BLOCK : (h + 1) * BLOCK]
            rows |= three(PER_HEAD * h + ROW_LSE, split3(-t))
            rows |= three(PER_HEAD * h + ROW_SPREAD, split3(-spreads[h][:, lane_block(i)]))
        rows |= {PER_HEAD * heads + s: carry_ref[s, i : i + 1, :] for s in range(2)}
        z_ref[chans:, lane_block(i)] = aug_rows(rows, BLOCK)
    rows = z_ref.shape[0]
    both_ref[:rows] = z_ref[...]
    part = reorder(dot_nt(att_ref[...].astype(BF16), full), count)
    high = part.astype(BF16)
    low = (part - high.astype(F32)).astype(BF16)
    for x, places in zip((high, low), part_places(part.shape, tokens, rows)):
        for i, (row, lanes) in enumerate(places):
            both_ref[row : row + AUG, lanes] = x[i * AUG : (i + 1) * AUG]
    for copy in copies:
        copy.wait()
    blocks = tokens // BLOCK

    def run(most):
        steps = range(EARLY[SIZES.index(most)] * blocks // 8)
        if steps:
            block_grads(
                steps, most, own_ref, z_ref, ka_ref, va_ref, kn_ref, dq_ref, acc_ref, slots_ref
            )

    by_need(slots_ref, run)


def part_places(shape, tokens, first):
    per_row = tokens // shape[1]
    tiles = shape[0] // AUG
    terms = []
    for _ in range(2):
        at = [divmod(i, per_row) for i in range(tiles)]
        terms.append(
            [(first + r * AUG, slice(c * shape[1], (c + 1) * shape[1])) for r, c in at]
        )
        first += -(-tiles // per_row) * AUG
    return terms


def parts_kernel(first, mine_ref, came_ref, out_ref):
    shape, tokens = out_ref.shape, mine_ref.shape[1]
    for tile, ends in enumerate(zip(*part_places(shape, tokens, first))):
        total = None
        for ref in (mine_ref, came_ref):
            terms = [ref[row : row + AUG, lanes].astype(F32) for row, lanes in ends]
            total = sum(terms) if total is None else total + sum(terms)
        out_ref[tile * AUG : (tile + 1) * AUG] = total


def query_side(q_ref, z_ref, here):
    chans = q_ref.shape[0]
    heads = chans // HEAD_DIM
    width = heads * BLOCK
    q_wide = spread_heads(q_ref[:, here], heads)
    g_wide = spread_heads(z_ref[:chans, here], heads)
    tile = z_ref[chans:, here].astype(F32)
    at = lax.broadcasted_iota(jnp.int32, tile.shape, 0)
    ones = jnp.logical_and(at >= ROW_BIAS, at < ROW_BIAS + 3)
    tiles = [tile] + [pltpu.roll(tile, AUG - PER_HEAD * h, 0) for h in range(1, heads)]
    aug = jnp.concatenate([jnp.where(ones, 1.0, x).astype(BF16) for x in tiles], axis=1)
    pad = jnp.zeros((BLOCK - chans - AUG, width), BF16)
    none = jnp.zeros((chans, width), BF16)
    q_aug = jnp.concatenate([q_wide, aug, pad], axis=0)
    g_aug = jnp.concatenate([g_wide, aug, pad], axis=0)
    q_out = jnp.concatenate([q_wide, none], axis=0)
    g_out = jnp.concatenate([none, g_wide], axis=0)
    return q_aug, g_aug, q_out, g_out


def products(side, slots, ka_ref, va_ref):
    q_aug, g_aug = side[:2]
    k_rows = jnp.concatenate([ka_ref[slot] for slot in slots], axis=0)
    v_rows = jnp.concatenate([va_ref[slot] for slot in slots], axis=0)
    probs = jnp.exp2(dot(k_rows, q_aug) * RAW)
    return probs.astype(BF16), (probs * dot(v_rows, g_aug)).astype(BF16)


def pair_grads(side, slots, probs, dlow, acc_ref):
    q_out, g_out = side[2:]
    both = dot_nt(probs, g_out) + dot_nt(dlow, q_out)
    for j, slot in enumerate(slots):
        acc_ref[slot] += both[j * BLOCK : (j + 1) * BLOCK]


def block_grads(steps, count, own_ref, z_ref, ka_ref, va_ref, kn_ref, dq_ref, acc_ref, slots_ref):
    heads = dq_ref.shape[0] // HEAD_DIM

    def begin(i):
        slots = [slots_ref[i, j] for j in range(count)]
        side = query_side(own_ref.at[2], z_ref, lane_block(i))
        return side, slots, *products(side, slots, ka_ref, va_ref)

    def finish(i, side, slots, probs, dlow):
        pair_grads(side, slots, probs, dlow, acc_ref)
        dq = dot(jnp.concatenate([kn_ref[slot] for slot in slots], axis=1), dlow)
        dq_ref[:, lane_block(i)] = (pick_heads(dq, heads) * SCALE).astype(BF16)

    in_order(steps, begin, finish, 1)


def grads_kernel(
    slots_vmem, own_ref, z_ref, ka_ref, va_ref, kn_ref, dq_in, acc_in,
    dq_ref, acc_ref, slots_ref, sems,
):
    copies = start_copies((slots_vmem,), (slots_ref,), sems)
    blocks = dq_ref.shape[1] // BLOCK
    for copy in copies:
        copy.wait()

    def run(most):
        steps = range(EARLY[SIZES.index(most)] * blocks // 8, blocks)
        block_grads(
            steps, most, own_ref, z_ref, ka_ref, va_ref, kn_ref, dq_ref, acc_ref, slots_ref
        )

    by_need(slots_ref, run)


def neighbours_kernel(
    dq_in, past_ref, pair_own, other_own, pair_ref, other_ref, ka_ref, va_ref,
    dq_ref, dk_ref, dv_ref, acc_ref, q_all, z_all, lists_vmem, todo_ref, lists_ref, sems,
):
    chans = dk_ref.shape[0]
    blocks = dk_ref.shape[1] // BLOCK
    ext = blocks + 2 * RIM
    odd = lax.rem(lax.axis_index("band"), 2) == 1
    for s, (ref, below) in enumerate(((pair_ref, odd), (other_ref, jnp.logical_not(odd)))):
        rows = ref[chans : chans + AUG].astype(F32)
        up = PER_HEAD * (chans // HEAD_DIM)
        row = jnp.where(below, rows[up : up + 1], rows[up + 1 : up + 2])
        for i in range(blocks):
            at = s * blocks + i
            lists_vmem[at : at + 1] = row[:, lane_block(i)].astype(jnp.int32)
    lists_vmem[2 * blocks :] = jnp.zeros_like(lists_vmem[2 * blocks :])
    copies = start_copies((lists_vmem,), (lists_ref,), sems)
    q_all[0] = pair_own[2]
    q_all[1] = other_own[2]
    z_all[0] = pair_ref[: z_all.shape[1]]
    z_all[1] = other_ref[...]
    dq_ref[...] = dq_in[...]
    for b in range(blocks):
        acc_ref[RIM + b] = past_ref[RIM + b]
    acc_ref[ext] = past_ref[ext]
    for copy in copies:
        copy.wait()
    step, many = 1, 9
    count = 0
    for row in range(2 * blocks):
        for c in range(0, MAX_KEYS, step):
            todo_ref[count] = row * MAX_KEYS + c
            count = count + (lists_ref[row, c] > 0).astype(jnp.int32)
    for j in range(many):
        todo_ref[count + j] = 2 * blocks * MAX_KEYS

    def body(k, carry):
        begun = []
        for j in range(many):
            todo = todo_ref[k * many + j]
            row, c = todo // MAX_KEYS, todo % MAX_KEYS
            here = pl.ds(pl.multiple_of(row % blocks * BLOCK, BLOCK), BLOCK)
            at = jnp.minimum(row // blocks, 1)
            side = query_side(q_all.at[at], z_all.at[at], here)
            slots = []
            for n in range(step):
                place_of = lists_ref[row, c + n]
                slots.append(jnp.where(place_of > 0, RIM - 1 + place_of, ext))
            begun.append((side, slots, *products(side, slots, ka_ref, va_ref)))
        for one in begun:
            pair_grads(*one, acc_ref)
        return carry

    lax.fori_loop(0, (count + many - 1) // many, body, 0)
    factor = part_factor(2 * chans)
    for b in range(blocks):
        x = (acc_ref[RIM + b] * factor).T
        dk_ref[:, lane_block(b)] = x[:chans].astype(BF16)
        dv_ref[:, lane_block(b)] = x[chans:].astype(BF16)


def part_factor(lanes):
    lane = lax.broadcasted_iota(jnp.int32, (BLOCK, lanes), 1)
    return jnp.where(lane < lanes // 2, SCALE, 1.0).astype(F32)


def kernel_call(body, outs, operands, scalars=(), scratch=(), flops=0, transcendentals=0, aliases=None):
    size = sum(x.size * x.dtype.itemsize for x in operands + outs)
    vmem = pl.BlockSpec(memory_space=pltpu.VMEM)
    copies = [pltpu.SMEM(x.shape, x.dtype) for x in scalars]
    if copies:
        copies.append(pltpu.SemaphoreType.DMA((len(copies),)))
    return pl.pallas_call(
        body,
        out_shape=outs,
        in_specs=[vmem] * len(operands),
        out_specs=[vmem] * len(outs),
        scratch_shapes=list(scratch) + copies,
        input_output_aliases=aliases or {},
        compiler_params=pltpu.CompilerParams(vmem_limit_bytes=VMEM_LIMIT),
        cost_estimate=pl.CostEstimate(
            flops=flops, bytes_accessed=size, transcendentals=transcendentals
        ),
    )(*operands)


def to_pair(value, axis):
    last = lax.axis_size(axis) - 1
    return lax.ppermute(value, axis, [(i, i ^ 1) for i in range(last + 1) if i ^ 1 <= last])


def to_other(value, axis):
    last = lax.axis_size(axis) - 1
    swap = [(i, ((i + 1) ^ 1) - 1) for i in range(last + 1)]
    return lax.ppermute(value, axis, [(i, j) for i, j in swap if 0 <= j <= last])


def gathered(value, axis):
    count = lax.axis_size(axis)
    if count & (count - 1):
        raise ValueError("axis size")
    step, parts = count // 2, {0: value}
    while step:
        swap = [(i, i ^ step) for i in range(count)]
        parts.update({m ^ step: lax.ppermute(x, axis, swap) for m, x in list(parts.items())})
        step //= 2
    return [parts[m] for m in range(count)]


class sum_steps:
    def __init__(self, value, axis):
        self.axis, self.count, self.value, self.came = axis, lax.axis_size(axis), value, None
        self.steps = [1 << i for i in range(self.count.bit_length() - 1)][:0:-1]

    def send(self):
        step = self.steps.pop(0)
        swap = [(i, i ^ step) for i in range(self.count)]
        self.came = lax.ppermute(self.value, self.axis, swap)

    def add(self):
        if self.came is not None:
            kind = BF16 if len(self.steps) == 1 else F32
            shape = jax.ShapeDtypeStruct(self.value.shape, kind)
            (self.value,) = kernel_call(add_kernel, [shape], [self.value, self.came])
            self.came = None


def shards(queries, keys, values, grad_out, w_out, key_lists, key_counts):
    chans, tokens = queries.shape
    blocks = tokens // BLOCK
    heads = chans // HEAD_DIM
    ext = blocks + 2 * RIM
    width = heads * BLOCK
    total = tokens * lax.axis_size("band")
    head_count = lax.axis_size("head")
    shape = jax.ShapeDtypeStruct
    pairs = blocks * MAX_KEYS * width * BLOCK

    if blocks != RIM or PER_HEAD * heads + 2 > AUG:
        raise ValueError("band size")
    like = lambda x: shape(x.shape, x.dtype)
    own = jnp.stack([keys, values, queries])
    other_own = to_other(own, "band")
    pair_own = to_pair(own, "band")
    parts = gathered(grad_out, "head")
    slots, carry, bias, acc, *state = kernel_call(
        functools.partial(prepare_kernel, total),
        [
            shape((blocks, BLOCK), jnp.int32),
            shape((2, blocks, BLOCK), F32),
            shape((3, ext, BLOCK), F32),
            shape((ext + 1, BLOCK, 2 * chans), F32),
            shape((ext + 1, BLOCK, BLOCK), BF16),
            shape((ext + 1, BLOCK, BLOCK), BF16),
            shape((ext + 1, chans, BLOCK), BF16),
            shape((ext + 1, chans + AUG, BLOCK), BF16),
        ],
        [own, key_lists, key_counts],
        [key_counts],
        scratch=[pltpu.VMEM((blocks, BLOCK), jnp.int32)],
    )
    ka, va, kn, vn, att, t = kernel_call(
        attend_kernel,
        [like(x) for x in state] + [shape((chans, tokens), F32), shape((blocks, width), F32)],
        [slots, own, bias, pair_own, other_own] + state,
        [slots],
        flops=3 * 2 * pairs * BLOCK,
        transcendentals=pairs,
        aliases={5 + i: i for i in range(4)},
    )
    z_rows = chans + AUG
    tail = [AUG + term[-1][0] for term in part_places(w_out.shape, tokens, z_rows)][-1]
    data = [ka, va, kn]
    operands = [slots, own, att, t, carry, w_out] + data + [acc]
    z, z_and_part, *done = kernel_call(
        functools.partial(project_kernel, head_count),
        [shape((z_rows, tokens), BF16), shape((tail, tokens), BF16), like(queries), like(acc)],
        operands + parts,
        [slots],
        flops=4 * w_out.size * tokens,
        aliases={len(operands) - 1: 3},
    )
    pair = to_pair(z_and_part, "band")
    other = to_other(z, "band")
    done, pair = lax.optimization_barrier((done, pair))
    (part_w,) = kernel_call(
        functools.partial(parts_kernel, z_rows), [shape(w_out.shape, F32)], [z_and_part, pair]
    )
    sums = sum_steps(part_w, "band")
    if sums.steps:
        sums.send()
        done, sums.value = lax.optimization_barrier((done, sums.value))
    done = kernel_call(
        grads_kernel,
        [like(x) for x in done],
        [slots, own, z] + data + list(done),
        [slots],
        flops=10 * pairs * BLOCK,
        transcendentals=pairs,
        aliases={6: 0, 7: 1},
    )
    if sums.steps:
        done, sums.came = lax.optimization_barrier((done, sums.came))
        sums.add()
        sums.send()
        done, sums.value = lax.optimization_barrier((done, sums.value))
    dq, dk, dv = kernel_call(
        neighbours_kernel,
        [shape((chans, tokens), BF16)] * 3,
        list(done) + [pair_own, other_own, pair, other, ka, va],
        scratch=[
            pltpu.VMEM(acc.shape, F32),
            pltpu.VMEM((2,) + queries.shape, BF16),
            pltpu.VMEM((2,) + z.shape, BF16),
            pltpu.VMEM((2 * blocks + 8, BLOCK), jnp.int32),
            pltpu.SMEM((2 * blocks * MAX_KEYS + 16,), jnp.int32),
            pltpu.SMEM((2 * blocks + 8, BLOCK), jnp.int32),
            pltpu.SemaphoreType.DMA((1,)),
        ],
        flops=4 * pairs * BLOCK,
        transcendentals=pairs // 2,
    )
    if sums.came is not None:
        dk, sums.came = lax.optimization_barrier((dk, sums.came))
    sums.add()
    while sums.steps:
        sums.send()
        sums.add()
    return (dq, dk, dv, sums.value)


def solution(mesh):
    in_specs = (
        P("head", "band"),
        P("head", "band"),
        P("head", "band"),
        P("head", "band"),
        P("head", None),
        P("band", None),
        P("band"),
    )
    out_specs = (P("head", "band"), P("head", "band"), P("head", "band"), P("head", None))
    return jax.shard_map(shards, mesh=mesh, in_specs=in_specs, out_specs=out_specs, check_vma=False)
```
